512 devices in a mesh: dp: 16 (over z, core), ctx: 4 (over x), enc: 8 (over y).
Axes of the slice: x: 4, y: 8, z: 8, core: 2. Of those that a mesh axis runs over, the one named last changes fastest.
Arguments:
- hidden: bfloat16 [16384, 4096], P(('dp', 'ctx')), may hold values from -16 to 16
- neighbour_states: bfloat16 [1536, 128, 896], P(('dp', 'ctx', 'enc')), may hold values from -16 to 16
- neighbour_owner: int32 [256, 2], P(('dp', 'ctx')), may hold values from 0 to 7, all different within a row; in each aligned block of 4 rows (0 to 3, 4 to 7, ...) at most 3 rows name the same one
- query_weight: bfloat16 [4096, 2048], P('dp', 'enc'), may hold values from -0.09375 to 0.09375
- key_weight: bfloat16 [896, 2048], P('dp', 'enc'), may hold values from -0.1875 to 0.1875
- value_weight: bfloat16 [896, 2048], P('dp', 'enc'), may hold values from -0.1875 to 0.1875
- out_weight: bfloat16 [2048, 4096], P('dp', 'enc'), may hold values from -0.5 to 0.5
- cotangent: bfloat16 [16384, 4096], P(('dp', 'ctx'), 'enc'), may hold values from -0.119628906 to 0.119628906
Outputs:
- mixed: bfloat16 [16384, 4096], P(('dp', 'ctx'), 'enc')
- grad_query_weight: float32 [4096, 2048], P('dp', 'enc')
The draws below stay inside these ranges and needn't reach their ends.
Inputs may be any that keep to these rules, and one draw needn't show every extreme that they name: `neighbour_owner`: the 2 neighbours of a span lie at different owners; within the rows of one device (4 spans, aligned blocks) no owner is named more than 3 times.
All inputs are finite; a program needn't handle non-finite values.
Results may differ from the reference program's by a relative error of at most 0.024.
Values may be sent and summed in bfloat16 or wider, within the bound.
A program may use at most 64 MiB of HBM per device.

```python
import math
import jax
import jax.numpy as jnp
import numpy as np
from jax import lax

D = 4096
ENC_D = 896
HEADS = 16
HEAD_DIM = 128
SPAN = 64
NEIGHBOURS = 2
NEIGH_LEN = 128
SPANS_DEV = 4
PROJ = 2048
SLOTS = 3
SEQ_LEN = 1024
TOKENS = 16384
ALL_SPANS = 256
ALL_SLOTS = 1536
N_DP = 16
N_CTX = 4
N_ENC = 8


def spread_rows(key, shape):
    base_key = jax.random.fold_in(jax.random.fold_in(key, 11), 0)
    values = jax.random.normal(base_key, shape, jnp.float32)
    return jnp.clip(values, -6.0, 6.0)


def draw_hidden(key, part):
    return spread_rows(key, (TOKENS, D)).astype(jnp.bfloat16)


def draw_neighbour_states(key, part):
    return spread_rows(jax.random.fold_in(key, 23), (ALL_SLOTS, NEIGH_LEN, ENC_D)).astype(jnp.bfloat16)


def shard_levels(rng, extent, cuts, least, top_value):
    factor_of, own = 1.0, jax.random.fold_in(rng, 6)
    for axis_at, blocks in cuts:
        draws = jnp.exp(jax.random.uniform(jax.random.fold_in(own, axis_at), (blocks,), jnp.float32, least / len(cuts), top_value / len(cuts)))
        factor_of = factor_of * jnp.repeat(draws, extent[axis_at] // blocks).reshape([-1 if axis == axis_at else 1 for axis in range(len(extent))])
    return factor_of


def routed_block(key, own, number, rows, amount, top, reach, slope):
    sequence = jax.random.permutation(key, amount)
    heavy_load, ordinary = portions_of(amount, rows * top, reach, slope, True), portions_of(amount, rows * top, reach, slope, False)
    places = jnp.arange(amount)

    def named(tallies, offset_by):
        used = int((tallies > 0).sum())
        fixed = max(1, used // 4)
        moved = fixed + (places - fixed + offset_by * (used - fixed)) % max(1, amount - fixed)
        return jnp.zeros((amount,), jnp.int32).at[sequence[jnp.where(places < fixed, places, moved)]].set(jnp.asarray(tallies, jnp.int32))

    tallies = jnp.where(number % 4 == 0, named(heavy_load, number // 4), named(ordinary, number - number // 4 - 1))
    mixed = jax.random.permutation(jax.random.fold_in(own, 3), amount)
    giver, taker = mixed[0:amount // 2 * 2:2], mixed[1:amount // 2 * 2:2]
    margin = jnp.minimum(tallies[giver] - 1, reach - tallies[taker]) // 2
    margin = jnp.where((giver == sequence[0]) | (taker == sequence[0]) | (tallies[taker] == 0), 0, jnp.maximum(margin, 0))
    moved = jax.random.randint(jax.random.fold_in(own, 4), (amount // 2,), 0, 1 << 20) % (margin + 1)
    tallies = tallies.at[giver].add(-moved).at[taker].add(moved)
    labels = jnp.searchsorted(jnp.cumsum(tallies), jnp.arange(rows * top), side="right").astype(jnp.int32)
    table = labels.reshape(top, rows).T
    table = table[jax.random.permutation(jax.random.fold_in(own, 1), rows)]
    offset_by = jax.random.randint(jax.random.fold_in(own, 2), (rows, 1), 0, top)
    return jnp.take_along_axis(table, (jnp.arange(top)[None, :] + offset_by) % top, axis=1)


def portions_of(amount, total, most, skew, full):
    weights = [(1 << 20) // math.isqrt(standing ** skew) + 1 for standing in range(1, amount + 1)]
    largest = most if full else min(most, max(-(-total // amount), total * weights[0] // sum(weights)))
    least = 1 if total - largest >= amount - 1 else 0
    counts, surplus = [largest] + [least] * (amount - 1), total - largest - least * (amount - 1)
    while surplus > 0:
        free = [i for i in range(1, amount) if counts[i] < largest] or [i for i in range(1, amount) if counts[i] < most]
        pool, left = sum([weights[i] for i in free]), surplus
        for i in free:
            extra = min(most - counts[i], max(1, left * weights[i] // pool), surplus)
            counts[i] = counts[i] + extra
            surplus = surplus - extra
    return np.array(counts)


def noise(rng, shape, deviation, limit, shards=(), kind=jnp.bfloat16):
    factor_of = shard_levels(rng, shape, shards, -0.22, 0.18) if shards else 1.0
    result = jax.random.normal(rng, shape, jnp.float32) * deviation * factor_of
    return jnp.minimum(jnp.maximum(result, -limit), limit).astype(kind)


def setup_inputs(seed: int = 0) -> dict:
    key_list = jax.random.split(jax.random.key(seed), 9)
    hidden = draw_hidden(jax.random.fold_in(key_list[8], 71), 0)
    neighbour_states = draw_neighbour_states(jax.random.fold_in(key_list[8], 71), 0)
    neighbour_owner_keys = jax.random.split(jax.random.fold_in(key_list[2], 1), ALL_SPANS // SPANS_DEV)
    neighbour_owner_turns = jax.random.permutation(jax.random.fold_in(key_list[2], 3), ALL_SPANS // SPANS_DEV)
    neighbour_owner = jax.vmap(lambda own, number: routed_block(jax.random.fold_in(key_list[2], 2), own, number, SPANS_DEV, N_ENC, NEIGHBOURS, SLOTS, 2))(neighbour_owner_keys, neighbour_owner_turns).reshape((ALL_SPANS, NEIGHBOURS))
    query_weight = noise(key_list[3], (D, PROJ), D ** -0.5, 0.09375, ((0, 16), (1, 8)))
    key_weight = noise(key_list[4], (ENC_D, PROJ), ENC_D ** -0.5, 0.1875, ((0, 16), (1, 8)))
    value_weight = noise(key_list[5], (ENC_D, PROJ), ENC_D ** -0.5, 0.1875, ((0, 16), (1, 8)))
    out_weight = noise(key_list[6], (PROJ, D), HEAD_DIM ** -0.5, 0.5, ((0, 16), (1, 8)))
    cotangent = noise(key_list[7], (TOKENS, D), 0.02, 0.119628906, ((0, 64), (1, 8)))
    return dict(hidden=hidden, neighbour_states=neighbour_states, neighbour_owner=neighbour_owner, query_weight=query_weight, key_weight=key_weight, value_weight=value_weight, out_weight=out_weight, cotangent=cotangent)


def slot_rows(neighbour_owner):
    groups = ALL_SPANS // SPANS_DEV
    flat_owner = neighbour_owner.reshape(groups, SPANS_DEV * NEIGHBOURS).astype(jnp.int32)
    owner_ids = jnp.arange(N_ENC, dtype=jnp.int32)
    onehot = (flat_owner[:, :, None] == owner_ids[None, None, :]).astype(jnp.int32)
    earlier = jnp.cumsum(onehot, axis=1) - onehot
    slot_rank = lax.optimization_barrier(jnp.sum(earlier * onehot, axis=2)).astype(jnp.int32)
    group_base = jnp.arange(groups, dtype=jnp.int32)[:, None] * (N_ENC * SLOTS)
    return (group_base + flat_owner * SLOTS + slot_rank).reshape(ALL_SPANS, NEIGHBOURS).astype(jnp.int32)

def shift_rows(matrix):
    tail_rows = jnp.zeros((SPAN - 1, matrix.shape[1]), matrix.dtype)
    joined = jnp.concatenate([matrix[SPAN - 1:], tail_rows], axis=0)
    return joined.reshape(SPANS_DEV * N_CTX, SPAN, HEADS, HEAD_DIM)

def unshift_rows(blocks):
    flat_rows = blocks.reshape(SPANS_DEV * N_CTX * SPAN, PROJ)
    head_rows = jnp.zeros((SPAN - 1, PROJ), flat_rows.dtype)
    return jnp.concatenate([head_rows, flat_rows[:SEQ_LEN - SPAN + 1]], axis=0)

def attention_grad(cotangent, out_weight):
    width = D // N_ENC
    total = jnp.zeros((SEQ_LEN, PROJ), jnp.float32)
    for block in range(N_ENC):
        cot_cols = cotangent[:, block * width:(block + 1) * width]
        out_cols = out_weight[:, block * width:(block + 1) * width]
        partial_sum = lax.dot_general(cot_cols, out_cols, (((1,), (1,)), ((), ())), preferred_element_type=jnp.float32)
        rounded = lax.optimization_barrier(partial_sum.astype(jnp.bfloat16))
        total = total + rounded.astype(jnp.float32)
    return total.astype(jnp.bfloat16)

def one_sequence(hidden, states, cotangent, query_weight, key_weight, value_weight, out_weight):
    inv_root = 1.0 / math.sqrt(HEAD_DIM)
    span_total = SPANS_DEV * N_CTX
    queries = jnp.dot(hidden, query_weight, preferred_element_type=jnp.float32).astype(jnp.bfloat16)
    flat_states = states.reshape(span_total * NEIGHBOURS * NEIGH_LEN, ENC_D)
    keys = jnp.dot(flat_states, key_weight, preferred_element_type=jnp.float32).astype(jnp.bfloat16)
    values = jnp.dot(flat_states, value_weight, preferred_element_type=jnp.float32).astype(jnp.bfloat16)
    keys = keys.reshape(span_total, NEIGHBOURS * NEIGH_LEN, HEADS, HEAD_DIM).astype(jnp.float32)
    values = values.reshape(span_total, NEIGHBOURS * NEIGH_LEN, HEADS, HEAD_DIM).astype(jnp.float32)
    grouped = shift_rows(queries).astype(jnp.float32)
    scores = jnp.einsum('cqhd,ckhd->chqk', grouped, keys) * inv_root
    probs = jax.nn.softmax(scores, axis=-1)
    rounded = probs.astype(jnp.bfloat16).astype(jnp.float32)
    blocks = jnp.einsum('chqk,ckhd->cqhd', rounded, values)
    attention = unshift_rows(blocks).astype(jnp.bfloat16)
    mixed = jnp.dot(attention, out_weight, preferred_element_type=jnp.float32).astype(jnp.bfloat16)
    grad_attention = attention_grad(cotangent, out_weight)
    grad_grouped = shift_rows(grad_attention).astype(jnp.float32)
    grad_probs = jnp.einsum('cqhd,ckhd->chqk', grad_grouped, values)
    inner = lax.optimization_barrier(jnp.sum(probs * grad_probs, axis=-1, keepdims=True))
    grad_scores = (probs * (grad_probs - inner)).astype(jnp.bfloat16).astype(jnp.float32)
    grad_blocks = jnp.einsum('chqk,ckhd->cqhd', grad_scores, keys) * inv_root
    grad_queries = unshift_rows(grad_blocks).astype(jnp.bfloat16)
    hidden_blocks = hidden.reshape(N_CTX, SPANS_DEV * SPAN, D).astype(jnp.float32)
    grad_blocks_rows = grad_queries.reshape(N_CTX, SPANS_DEV * SPAN, PROJ).astype(jnp.float32)
    parts = jnp.einsum('ntd,ntp->ndp', hidden_blocks, grad_blocks_rows).astype(jnp.bfloat16)
    return (mixed, lax.optimization_barrier(jnp.sum(parts.astype(jnp.float32), axis=0)))

def reference(hidden, neighbour_states, neighbour_owner, query_weight, key_weight, value_weight, out_weight, cotangent):
    rows = slot_rows(neighbour_owner).reshape(N_DP, SPANS_DEV * N_CTX, NEIGHBOURS)
    hidden_seq = hidden.reshape(N_DP, SEQ_LEN, D)
    cotangent_seq = cotangent.reshape(N_DP, SEQ_LEN, D)

    def advance(running, items):
        hidden_one, rows_one, cotangent_one = items
        states = jnp.take(neighbour_states, rows_one.reshape(-1), axis=0)
        mixed_one, grad_one = one_sequence(hidden_one, states, cotangent_one, query_weight, key_weight, value_weight, out_weight)
        return (running + grad_one, mixed_one)
    running, mixed = lax.scan(advance, jnp.zeros((D, PROJ), jnp.float32), (hidden_seq, rows, cotangent_seq))
    return (mixed.reshape(TOKENS, D), running)
```

```python
import functools
import math

import jax
import jax.numpy as jnp
from jax import lax
from jax.experimental import pallas as pl
from jax.experimental.pallas import tpu as pltpu
from jax.sharding import PartitionSpec as P

HEAD_DIM = 128
MESH = pl.DeviceIdType.MESH
BF16 = jnp.bfloat16
F32 = jnp.float32
NT = (((1,), (1,)), ((), ()))


def dot(a, b, dims=(((1,), (0,)), ((), ()))):
    return lax.dot_general(a, b, dims, preferred_element_type=F32)


def rows_of(ref, index, count):
    step = 128 if count % 128 == 0 else 16
    return ref.at[pl.ds(pl.multiple_of(index * count, step), count)]


class Ring:
    def __init__(self, buf, slot, first, send, recv, right, left, own=None):
        self.buf, self.slot = buf, slot
        self.first, self.send, self.recv = first, send, recv
        self.right, self.left, self.own = right, left, own
        self.sent = []

    def part(self, ref, half):
        if half == 0:
            return ref.at[pl.ds(0, self.first)]
        return ref.at[pl.ds(self.first, ref.shape[0] - self.first)]

    def start(self, step, last):
        for way, to, sign in ((0, self.right, -1), (1, self.left, 1)):
            dst = self.slot(sign * (step - 1))
            src = self.own if step == 1 and self.own is not None else dst
            if step == last:
                src, dst = self.part(src, way), self.part(dst, way)
            copy = pltpu.make_async_remote_copy(
                src_ref=src,
                dst_ref=dst,
                send_sem=self.send.at[way, step - 1],
                recv_sem=self.recv.at[way, step - 1],
                device_id=to,
                device_id_type=MESH,
            )
            copy.start()
            self.sent.append(copy)

    def wait(self, step, last):
        for way, sign in ((0, -1), (1, 1)):
            dst = self.slot(sign * step)
            if step == last:
                dst = self.part(dst, way)
            pltpu.make_async_remote_copy(
                src_ref=dst,
                dst_ref=dst,
                send_sem=self.send.at[way, step - 1],
                recv_sem=self.recv.at[way, step - 1],
                device_id=self.right,
                device_id_type=MESH,
            ).wait_recv()


def kernel(
    cores, nz, nx, ny, spans, hid_h, st_h, owner, wq_h, wk_v, wv_v, wo_h, cot_h, mixed_o, grad_o,
    hid, cot, wq, wo, wkv, kvw_f, kvw, a2a, picked, kv, gpart, rs_out, rs_in, qpad, gpad, probs,
    apad, att, gqpad, gqt, sib_out, sib_in, xs, x_in, zs, z_in, fin, acc,
    local_sem, a2a_s, a2a_r, pick_s, pick_r, rs_s, rs_r, att_s, att_r,
    wo_s, wo_r, wq_s, wq_r, kw_s, kw_r, wo_cs, wo_cr, wq_cs, wq_cr, kw_cs, kw_cr,
    halo_s, halo_r, sib_s, sib_r, x_s, x_r, z_s, z_r, f_s, f_r,
):
    dp, x, y = lax.axis_index("dp"), lax.axis_index("ctx"), lax.axis_index("enc")
    z, core = lax.div(dp, cores), lax.rem(dp, cores)
    sib = {"dp": z * cores + (1 - core)}

    def zat(k):
        return lax.rem(z + (k + nz), nz)

    def xat(k):
        return lax.rem(x + (k + nx), nx)

    def yat(k):
        return lax.rem(y + (k + ny), ny)

    def zdev(k):
        return {"dp": zat(k) * cores + core}

    def xdev(k):
        return {"ctx": xat(k)}

    def ydev(k):
        return {"enc": yat(k)}

    hy, hz = ny // 2, nz // 2
    tok = hid.shape[0]
    proj = wq.shape[1]
    heads = proj // HEAD_DIM
    span = tok // spans
    pairs = picked.shape[1]
    used = owner.shape[0] * owner.shape[1]
    piece = pairs // used
    scale = 1.0 / math.sqrt(HEAD_DIM)
    sent = []

    def remote(src, dst, s, r, to, start=True):
        copy = pltpu.make_async_remote_copy(
            src_ref=src, dst_ref=dst, send_sem=s, recv_sem=r, device_id=to, device_id_type=MESH
        )
        if start:
            copy.start()
            sent.append(copy)
        return copy

    with jax.named_scope("entry"):
        barrier = pltpu.get_barrier_semaphore()
        peers = [sib]
        peers += [ydev(k) for k in range(1, ny)]
        peers += [xdev(k) for k in range(1, nx)]
        peers += [zdev(k) for k in range(1, nz)]
        for peer in peers:
            pl.semaphore_signal(barrier, inc=1, device_id=peer, device_id_type=MESH)

        local = [
            pltpu.make_async_copy(st_h.at[:, pl.ds(pl.multiple_of(y * piece, 16), piece), :], a2a.at[y], local_sem.at[0]),
            pltpu.make_async_copy(wo_h, rows_of(wo, dp, wo_h.shape[0]), local_sem.at[1]),
            pltpu.make_async_copy(wq_h, rows_of(wq, dp, wq_h.shape[0]), local_sem.at[2]),
            pltpu.make_async_copy(cot_h, cot, local_sem.at[3]),
            pltpu.make_async_copy(hid_h, hid, local_sem.at[4]),
        ]
        for copy in local:
            copy.start()
        kw_rows = wk_v.shape[0]
        rows_of(wkv, dp, 2 * kw_rows)[...] = jnp.concatenate(
            [wk_v[...].astype(F32), wv_v[...].astype(F32)], axis=0
        ).astype(BF16)
        qpad[...] = jnp.zeros_like(qpad)
        gpad[...] = jnp.zeros_like(gpad)
        pl.semaphore_wait(barrier, len(peers))

    def weight_ring(buf, own, first, s, r):
        rows = buf.shape[0] // (cores * nz)
        return Ring(buf, lambda k: rows_of(buf, zat(k) * cores + core, rows), first, s, r, zdev(1), zdev(-1), own)

    wo_ring = weight_ring(wo, wo_h, wo_h.shape[0] // 2, wo_s, wo_r)
    wq_ring = weight_ring(wq, wq_h, wq_h.shape[0] // 2, wq_s, wq_r)
    kw_ring = weight_ring(wkv, None, 64, kw_s, kw_r)
    weights = ((wo_ring, wo_cs, wo_cr), (kw_ring, kw_cs, kw_cr), (wq_ring, wq_cs, wq_cr))

    def pass_on(k):
        for ring, s, r in weights:
            block = ring.slot(k)
            src = ring.own if k == 0 and ring.own is not None else block
            remote(src, block, s.at[k % nz], r.at[k % nz], sib)

    def from_sibling(ring, s, r, buf):
        rows = buf.shape[0] // (cores * nz)
        for k in range(nz):
            block = rows_of(buf, zat(k) * cores + (1 - core), rows)
            remote(block, block, s.at[k], r.at[k], sib, start=False).wait_recv()

    with jax.named_scope("spread"):
        for k in sorted(range(1, ny), key=lambda k: -min(k, ny - k)):
            to = yat(k)
            remote(
                st_h.at[:, pl.ds(pl.multiple_of(to * piece, 16), piece), :],
                a2a.at[y], a2a_s.at[k - 1], a2a_r.at[k - 1], ydev(k),
            )
        for ring, _, _ in weights:
            ring.start(1, hz)
        pass_on(0)

    def weight_step(step):
        for ring, _, _ in weights:
            ring.wait(step, hz)
            if step < hz:
                ring.start(step + 1, hz)
        pass_on(step)
        if step < hz:
            pass_on(-step)

    with jax.named_scope("weights_1_2"):
        weight_step(1)
        weight_step(2)

    pick_ring = Ring(
        picked, lambda k: picked.at[yat(k)], pairs // 2, pick_s, pick_r, ydev(1), ydev(-1)
    )
    with jax.named_scope("select"):
        for k in range(1, ny):
            block = a2a.at[yat(-k)]
            remote(block, block, a2a_s.at[k - 1], a2a_r.at[k - 1], ydev(k), start=False).wait_recv()
        local[0].wait()
        names = [owner[i // owner.shape[1], i % owner.shape[1]] for i in range(used)]
        for i in range(used):
            rank = sum([(names[i] == names[j]).astype(jnp.int32) for j in range(i)], jnp.int32(0))
            picked[y, i * piece : (i + 1) * piece, :] = a2a[names[i], jnp.minimum(rank, a2a.shape[1] - 1)]
        pick_ring.start(1, hy)

    with jax.named_scope("weights_3"):
        weight_step(3)
    with jax.named_scope("picked_1"):
        pick_ring.wait(1, hy)
        pick_ring.start(2, hy)
    with jax.named_scope("weights_4"):
        weight_step(4)
    with jax.named_scope("unpack"):
        local[1].wait()
        from_sibling(*weights[0], wo)
        from_sibling(*weights[1], wkv)
        for i in range(cores * nz):
            both = wkv[2 * kw_rows * i : 2 * kw_rows * (i + 1), :].astype(F32)
            kvw_f[kw_rows * i : kw_rows * (i + 1), :proj] = both[:kw_rows]
            kvw_f[kw_rows * i : kw_rows * (i + 1), proj:] = both[kw_rows:]
        kvw[...] = kvw_f[...].astype(BF16)

    per_span = pairs // spans

    def project(k):
        place = yat(k)
        made = dot(picked[place], kvw[...]).astype(BF16)
        at = pl.ds(pl.multiple_of(place * per_span, 16), per_span)
        for u in range(spans):
            kv[1 + u, at, :] = made[u * per_span : (u + 1) * per_span]
        remote(kv.at[spans, at], kv.at[0, at], halo_s.at[k % ny], halo_r.at[k % ny], xdev(1))

    with jax.named_scope("grad_partial"):
        local[3].wait()

        def partial(k):
            rows = rows_of(wo, yat(k), proj)
            gpart[k % ny] = dot(cot[...], rows[...], NT).astype(BF16)

        for k in range(ny):
            partial(hy - k)

    def rs_start(step):
        for way, to in ((0, ydev(1)), (1, ydev(-1))):
            src, dst = rs_out.at[way, step - 1], rs_in.at[way, step - 1]
            if step == 1:
                half = pl.ds(way * (tok // 2), tok // 2)
                src, dst = gpart.at[hy, half], rs_in.at[way, 0, half]
            remote(src, dst, rs_s.at[way, step - 1], rs_r.at[way, step - 1], to)

    def rs_wait(step):
        for way in range(2):
            dst = rs_in.at[way, step - 1]
            if step == 1:
                dst = rs_in.at[way, 0, pl.ds(way * (tok // 2), tok // 2)]
            remote(dst, dst, rs_s.at[way, step - 1], rs_r.at[way, step - 1], ydev(1), start=False).wait_recv()

    def rs_step(step):
        rs_wait(step)
        left = hy - step
        for way, k in ((0, left), (1, ny - left)):
            if step == 1:
                lo, hi = way * (tok // 2), (way + 1) * (tok // 2)
                rs_out[way, step, lo:hi] = (
                    rs_in[way, 0, lo:hi].astype(F32) + gpart[k, lo:hi].astype(F32)
                ).astype(BF16)
                lo, hi = (1 - way) * (tok // 2), (2 - way) * (tok // 2)
                rs_out[way, step, lo:hi] = gpart[k, lo:hi]
            else:
                rs_out[way, step] = (
                    rs_in[way, step - 1].astype(F32) + gpart[k].astype(F32)
                ).astype(BF16)
        rs_start(step + 1)

    with jax.named_scope("rs_1"):
        rs_start(1)
        project(0)
        project(1)
        project(-1)
    with jax.named_scope("picked_2"):
        pick_ring.wait(2, hy)
        pick_ring.start(3, hy)
        project(2)
        project(-2)
    with jax.named_scope("queries"):
        local[2].wait()
        local[4].wait()
        from_sibling(*weights[2], wq)
        qpad[pl.ds(1, tok), :] = dot(hid[...], wq[...]).astype(BF16).astype(F32)
    with jax.named_scope("picked_3"):
        pick_ring.wait(3, hy)
        pick_ring.start(4, hy)
        project(3)
        project(-3)
    with jax.named_scope("rs_2"):
        rs_step(1)
    with jax.named_scope("picked_4"):
        pick_ring.wait(4, hy)
        project(4)
    with jax.named_scope("rs_3"):
        rs_step(2)

    def forward(g):
        rows = pl.ds(g * span, span)
        for h in range(heads):
            cols = pl.ds(h * HEAD_DIM, HEAD_DIM)
            q = qpad[rows, cols].astype(BF16)
            scores = dot(q, kv[g, :, cols], NT) * scale
            e = jnp.exp(scores - jnp.max(scores, axis=-1, keepdims=True))
            p = e / jnp.sum(e, axis=-1, keepdims=True)
            probs[g * heads + h] = p
            out = dot(p.astype(BF16), kv[g, :, pl.ds(proj + h * HEAD_DIM, HEAD_DIM)])
            if g == 0:
                out = jnp.where(x == 0, jnp.zeros_like(out), out)
            apad[rows, cols] = out

    with jax.named_scope("forward"):
        for g in range(1, spans + 1):
            forward(g)
    with jax.named_scope("rs_4"):
        rs_step(3)
    with jax.named_scope("halo"):
        for k in range(ny):
            at = pl.ds(pl.multiple_of(yat(k) * per_span, 16), per_span)
            remote(kv.at[0, at], kv.at[0, at], halo_s.at[k], halo_r.at[k], xdev(1), start=False).wait_recv()
        forward(0)
    att_ring = Ring(att, lambda k: att.at[yat(k)], tok // 2, att_s, att_r, ydev(1), ydev(-1))
    with jax.named_scope("att_1"):
        att[y] = apad[pl.ds(1, tok), :].astype(BF16)
        att_ring.start(1, hy)
    with jax.named_scope("rs_last"):
        rs_wait(hy)
        total = gpart[0].astype(F32) + rs_in[0, hy - 1].astype(F32) + rs_in[1, hy - 1].astype(F32)
        gpad[pl.ds(1, tok), :] = total.astype(BF16).astype(F32)

    def backward(g):
        rows = pl.ds(g * span, span)
        for h in range(heads):
            cols = pl.ds(h * HEAD_DIM, HEAD_DIM)
            p = probs[g * heads + h]
            gp = dot(gpad[rows, cols].astype(BF16), kv[g, :, pl.ds(proj + h * HEAD_DIM, HEAD_DIM)], NT)
            gs = (p * (gp - jnp.sum(p * gp, axis=-1, keepdims=True))).astype(BF16)
            out = dot(gs, kv[g, :, cols]) * scale
            if g == 0:
                out = jnp.where(x == 0, jnp.zeros_like(out), out)
            gqpad[rows, cols] = out

    with jax.named_scope("backward"):
        for g in range(spans + 1):
            backward(g)
        gqt[...] = gqpad[pl.ds(1, tok), :].astype(BF16).astype(F32).T.astype(BF16)

    wide = grad_o.shape[0]

    def weight_grad(p, c):
        block = zat(p + 1) * cores + c
        return dot(gqt[...], hid[:, pl.ds(pl.multiple_of(block * wide, 128), wide)])

    with jax.named_scope("to_sibling"):
        for p in range(nz):
            sib_out[p] = weight_grad(p, 1 - core).astype(BF16)
            remote(sib_out.at[p], sib_in.at[p], sib_s.at[p], sib_r.at[p], sib)
    with jax.named_scope("att_2"):
        att_ring.wait(1, hy)
        att_ring.start(2, hy)

    quarter = proj // nx
    batch = nz // 2

    def x_copy(b, k, start):
        to = pl.ds(pl.multiple_of(xat(k) * quarter, 16), quarter)
        return remote(
            xs.at[pl.ds(b * batch, batch), to], x_in.at[k - 1, pl.ds(b * batch, batch)],
            x_s.at[b, k - 1], x_r.at[b, k - 1], xdev(k), start,
        )

    with jax.named_scope("to_x"):
        for p in range(nz):
            mine = weight_grad(p, core).astype(BF16).astype(F32)
            remote(sib_in.at[p], sib_in.at[p], sib_s.at[p], sib_r.at[p], sib, start=False).wait_recv()
            xs[p] = (mine + sib_in[p].astype(F32)).astype(BF16)
            if p % batch == batch - 1:
                for k in range(1, nx):
                    x_copy(p // batch, k, True)

    def mix(k):
        rows = rows_of(wo, yat(k), proj)
        made = dot(att[yat(k)], rows[...])
        if k == 0:
            acc[...] = made
        else:
            acc[...] += made

    with jax.named_scope("att_3"):
        att_ring.wait(2, hy)
        att_ring.start(3, hy)
        mix(0)
        mix(1)
        mix(-1)

    own_quarter = pl.ds(pl.multiple_of(x * quarter, 16), quarter)

    def z_send(b):
        for k in range(1, nx):
            x_copy(b, k, False).wait_recv()
        for p in range(b * batch, (b + 1) * batch):
            total = xs[p, own_quarter, :].astype(F32)
            for k in range(1, nx):
                total += x_in[k - 1, p].astype(F32)
            zs[p] = total.astype(BF16)
            if p + 1 < nz:
                remote(zs.at[p], z_in.at[p], z_s.at[p], z_r.at[p], zdev(p + 1))

    with jax.named_scope("to_z"):
        z_send(0)
    with jax.named_scope("att_4"):
        att_ring.wait(3, hy)
        att_ring.start(4, hy)
        mix(2)
        mix(-2)
    with jax.named_scope("to_z_2"):
        z_send(1)
        mix(3)
        mix(-3)
    with jax.named_scope("from_z"):
        total = zs[nz - 1].astype(F32)
        for p in range(nz - 1):
            remote(zs.at[p], z_in.at[p], z_s.at[p], z_r.at[p], zdev(p + 1), start=False).wait_recv()
            total += z_in[p].astype(F32)
        fin[x] = total.astype(BF16)
        for k in range(1, nx):
            remote(fin.at[x], fin.at[x], f_s.at[k - 1], f_r.at[k - 1], xdev(k))
    with jax.named_scope("mixed"):
        att_ring.wait(4, hy)
        mix(4)
        mixed_o[...] = acc[...].astype(BF16)
    with jax.named_scope("from_x"):
        for k in range(1, nx):
            block = fin.at[xat(-k)]
            remote(block, block, f_s.at[k - 1], f_r.at[k - 1], xdev(k), start=False).wait_recv()
        grad_o[...] = fin[...].astype(F32).reshape(proj, wide).T
    with jax.named_scope("drain"):
        for copy in sent + wo_ring.sent + wq_ring.sent + kw_ring.sent + pick_ring.sent + att_ring.sent:
            copy.wait_send()


def shards(sizes, hidden, states, owner, query_w, key_w, value_w, out_w, cotangent):
    cores, nz, nx, ny = sizes
    tok, wide = hidden.shape
    slots, length, enc_d = states.shape
    spans, per = owner.shape
    proj = query_w.shape[1]
    heads = proj // HEAD_DIM
    n_dp = cores * nz
    used = spans * per
    piece = length // ny
    pairs = used * piece
    cols = out_w.shape[1]
    keys = per * length
    padded = tok + tok // spans
    dma = pltpu.SemaphoreType.DMA
    any_, vmem = pl.BlockSpec(memory_space=pl.ANY), pl.BlockSpec(memory_space=pltpu.VMEM)
    quarter = proj // nx
    scratch = [
        pltpu.VMEM((tok, wide), BF16),
        pltpu.VMEM((tok, cols), BF16),
        pltpu.VMEM((wide, proj), BF16),
        pltpu.VMEM((n_dp * out_w.shape[0], cols), BF16),
        pltpu.VMEM((2 * enc_d, proj), BF16),
        pltpu.VMEM((enc_d, 2 * proj), F32),
        pltpu.VMEM((enc_d, 2 * proj), BF16),
        pltpu.VMEM((ny, slots, piece, enc_d), BF16),
        pltpu.VMEM((ny, pairs, enc_d), BF16),
        pltpu.VMEM((spans + 1, keys, 2 * proj), BF16),
        pltpu.VMEM((ny, tok, proj), BF16),
        pltpu.VMEM((2, ny // 2, tok, proj), BF16),
        pltpu.VMEM((2, ny // 2, tok, proj), BF16),
        pltpu.VMEM((padded, proj), F32),
        pltpu.VMEM((padded, proj), F32),
        pltpu.VMEM(((spans + 1) * heads, tok // spans, keys), F32),
        pltpu.VMEM((padded, proj), F32),
        pltpu.VMEM((ny, tok, proj), BF16),
        pltpu.VMEM((padded, proj), F32),
        pltpu.VMEM((proj, tok), BF16),
        pltpu.VMEM((nz, proj, wide // n_dp), BF16),
        pltpu.VMEM((nz, proj, wide // n_dp), BF16),
        pltpu.VMEM((nz, proj, wide // n_dp), BF16),
        pltpu.VMEM((nx - 1, nz, quarter, wide // n_dp), BF16),
        pltpu.VMEM((nz, quarter, wide // n_dp), BF16),
        pltpu.VMEM((nz - 1, quarter, wide // n_dp), BF16),
        pltpu.VMEM((nx, quarter, wide // n_dp), BF16),
        pltpu.VMEM((tok, cols), F32),
        dma((5,)),
        dma((ny - 1,)), dma((ny - 1,)),
        dma((2, ny // 2)), dma((2, ny // 2)),
        dma((2, ny // 2)), dma((2, ny // 2)),
        dma((2, ny // 2)), dma((2, ny // 2)),
        dma((2, nz // 2)), dma((2, nz // 2)),
        dma((2, nz // 2)), dma((2, nz // 2)),
        dma((2, nz // 2)), dma((2, nz // 2)),
        dma((nz,)), dma((nz,)), dma((nz,)), dma((nz,)), dma((nz,)), dma((nz,)),
        dma((ny,)), dma((ny,)),
        dma((nz,)), dma((nz,)),
        dma((2, nx - 1)), dma((2, nx - 1)),
        dma((nz - 1,)), dma((nz - 1,)),
        dma((nx - 1,)), dma((nx - 1,)),
    ]
    return pl.pallas_call(
        functools.partial(kernel, cores, nz, nx, ny, spans),
        out_shape=(
            jax.ShapeDtypeStruct((tok, cols), BF16),
            jax.ShapeDtypeStruct((wide // n_dp, proj), F32),
        ),
        in_specs=[any_, any_, pl.BlockSpec(memory_space=pltpu.SMEM), any_, vmem, vmem, any_, any_],
        out_specs=(vmem, vmem),
        scratch_shapes=scratch,
        compiler_params=pltpu.CompilerParams(
            collective_id=0, has_side_effects=True, vmem_limit_bytes=48 * 2**20
        ),
        cost_estimate=pl.CostEstimate(flops=3 * 10**9, bytes_accessed=8 * 2**20, transcendentals=163840),
    )(hidden, states, owner, query_w, key_w, value_w, out_w, cotangent)


def solution(mesh):
    sizes = (2, mesh.shape["dp"] // 2, mesh.shape["ctx"], mesh.shape["enc"])
    in_specs = (
        P(("dp", "ctx"), None),
        P(("dp", "ctx", "enc"), None, None),
        P(("dp", "ctx"), None),
        P("dp", "enc"),
        P("dp", "enc"),
        P("dp", "enc"),
        P("dp", "enc"),
        P(("dp", "ctx"), "enc"),
    )
    out_specs = (P(("dp", "ctx"), "enc"), P("dp", "enc"))
    return jax.shard_map(
        functools.partial(shards, sizes),
        mesh=mesh,
        in_specs=in_specs,
        out_specs=out_specs,
        check_vma=False,
    )
```

```python
import functools
import math

import jax
import jax.numpy as jnp
from jax import lax
from jax.experimental import pallas as pl
from jax.experimental.pallas import tpu as pltpu
from jax.sharding import PartitionSpec as P

HEAD_DIM = 128
MESH = pl.DeviceIdType.MESH
BF16 = jnp.bfloat16
F32 = jnp.float32
NT = (((1,), (1,)), ((), ()))


def dot(a, b, dims=(((1,), (0,)), ((), ()))):
    return lax.dot_general(a, b, dims, preferred_element_type=F32)


def rows_of(ref, index, count):
    step = 128 if count % 128 == 0 else 16
    return ref.at[pl.ds(pl.multiple_of(index * count, step), count)]


class Ring:
    def __init__(self, slot, first, send, recv, right, left, own=None, number=0):
        self.slot, self.number = slot, number
        self.first, self.send, self.recv = first, send, recv
        self.right, self.left, self.own = right, left, own
        self.sent = []

    def part(self, ref, half):
        if half == 0:
            return ref.at[pl.ds(0, self.first)]
        return ref.at[pl.ds(self.first, ref.shape[0] - self.first)]

    def start(self, step, last):
        for way, to, sign in ((0, self.right, -1), (1, self.left, 1)):
            dst = self.slot(sign * (step - 1))
            src = self.own if step == 1 and self.own is not None else dst
            if step == last:
                src, dst = self.part(src, way), self.part(dst, way)
            copy = pltpu.make_async_remote_copy(
                src_ref=src,
                dst_ref=dst,
                send_sem=self.send.at[way, step - 1],
                recv_sem=self.recv.at[way, step - 1],
                device_id=to,
                device_id_type=MESH,
            )
            copy.start()
            self.sent.append(copy)

    def wait(self, step, last):
        for way, sign in ((0, -1), (1, 1)):
            dst = self.slot(sign * step)
            if step == last:
                dst = self.part(dst, way)
            pltpu.make_async_remote_copy(
                src_ref=dst,
                dst_ref=dst,
                send_sem=self.send.at[way, step - 1],
                recv_sem=self.recv.at[way, step - 1],
                device_id=self.right,
                device_id_type=MESH,
            ).wait_recv()


def kernel(
    cores, nz, nx, ny, spans, hid_h, st_h, owner, wq_h, wk_h, wv_h, wo_h, cot_h, mixed_o, grad_o,
    hid, cot, wk_v, wv_v, wq, wo, wkv, kvw_f, kvw, a2a, picked, kv, gpart, rs_out, rs_in, qpad, gpad, probs,
    apad, att, gqpad, ht, hx, gq, part, sib_out, sib_in, zs, z_in, fin, acc,
    local_sem, a2a_s, a2a_r, pick_s, pick_r, rs_s, rs_r, att_s, att_r,
    wo_s, wo_r, wq_s, wq_r, kw_s, kw_r, wo_cs, wo_cr, wq_cs, wq_cr, kw_cs, kw_cr, wq_xs, wq_xr,
    halo_s, halo_r, hx_s, hx_r, gq_s, gq_r, sib_s, sib_r, z_s, z_r, f_s, f_r,
):
    dp, x, y = lax.axis_index("dp"), lax.axis_index("ctx"), lax.axis_index("enc")
    z, core = lax.div(dp, cores), lax.rem(dp, cores)
    sib = {"dp": z * cores + (1 - core)}

    def zat(k):
        return lax.rem(z + (k + nz), nz)

    def xat(k):
        return lax.rem(x + (k + nx), nx)

    def yat(k):
        return lax.rem(y + (k + ny), ny)

    def zdev(k):
        return {"dp": zat(k) * cores + core}

    def xdev(k):
        return {"ctx": xat(k)}

    def ydev(k):
        return {"enc": yat(k)}

    hy, hz = ny // 2, nz // 2
    tok = hid.shape[0]
    proj = wq_h.shape[1]
    wide = wq_h.shape[0]
    quarter = wide // nx
    heads = proj // HEAD_DIM
    span = tok // spans
    pairs = picked.shape[1]
    used = owner.shape[0] * owner.shape[1]
    piece = pairs // used
    kw_rows = wk_v.shape[0]
    scale = 1.0 / math.sqrt(HEAD_DIM)
    sent = []

    def remote(src, dst, s, r, to, start=True):
        copy = pltpu.make_async_remote_copy(
            src_ref=src, dst_ref=dst, send_sem=s, recv_sem=r, device_id=to, device_id_type=MESH
        )
        if start:
            copy.start()
            sent.append(copy)
        return copy

    with jax.named_scope("entry"):
        barrier = pltpu.get_barrier_semaphore()
        peers = [sib]
        peers += [ydev(k) for k in range(1, ny)]
        peers += [xdev(k) for k in range(1, nx)]
        peers += [zdev(k) for k in range(1, nz)]
        for peer in peers:
            pl.semaphore_signal(barrier, inc=1, device_id=peer, device_id_type=MESH)

        local = [
            pltpu.make_async_copy(st_h.at[:, pl.ds(pl.multiple_of(y * piece, 16), piece), :], a2a.at[y], local_sem.at[0]),
            pltpu.make_async_copy(wo_h, rows_of(wo, dp, wo_h.shape[0]), local_sem.at[1]),
            pltpu.make_async_copy(wq_h, wq.at[z, core], local_sem.at[2]),
            pltpu.make_async_copy(cot_h, cot, local_sem.at[3]),
            pltpu.make_async_copy(hid_h, hid, local_sem.at[4]),
            pltpu.make_async_copy(wk_h, wk_v, local_sem.at[5]),
            pltpu.make_async_copy(wv_h, wv_v, local_sem.at[6]),
        ]
        for copy in local:
            copy.start()
        local[5].wait()
        local[6].wait()
        rows_of(wkv, dp, 2 * kw_rows)[...] = jnp.concatenate(
            [wk_v[...].astype(F32), wv_v[...].astype(F32)], axis=0
        ).astype(BF16)
        qpad[...] = jnp.zeros_like(qpad)
        gpad[...] = jnp.zeros_like(gpad)
        pl.semaphore_wait(barrier, len(peers))

    class Weight:
        def __init__(self, buf, own, cuts, s, r, to_sib, from_sib):
            self.rows = buf.shape[0] // (cores * nz)
            self.buf, self.own, self.s, self.r = buf, own, to_sib, from_sib
            self.rings = []
            for n, (lo, hi) in enumerate(zip(cuts, [*cuts[1:], self.rows])):
                part = pl.ds(lo, hi - lo)
                self.rings.append(
                    Ring(
                        lambda k, part=part: self.block(k, core).at[part],
                        (hi - lo + 16) // 32 * 16, s.at[n], r.at[n], zdev(1), zdev(-1),
                        None if own is None else own.at[part],
                    )
                )

        def block(self, k, c):
            return rows_of(self.buf, zat(k) * cores + c, self.rows)

        def start(self):
            for ring in self.rings:
                ring.start(1, hz)
            self.pass_on(0)

        def pass_on(self, k):
            block = self.block(k, core)
            src = self.own if k == 0 and self.own is not None else block
            remote(src, block, self.s.at[k % nz], self.r.at[k % nz], sib)

        def wait(self, step):
            for ring in self.rings:
                ring.wait(step, hz)
                if step < hz:
                    ring.start(step + 1, hz)
            self.pass_on(step)
            if step < hz:
                self.pass_on(-step)

        def from_sibling(self):
            for k in range(nz):
                block = self.block(k, 1 - core)
                remote(block, block, self.s.at[k], self.r.at[k], sib, start=False).wait_recv()

    out_w = Weight(wo, wo_h, (0, wo_h.shape[0] // 2), wo_s, wo_r, wo_cs, wo_cr)
    kv_w = Weight(wkv, None, (0,), kw_s, kw_r, kw_cs, kw_cr)

    def query_piece(k, q):
        return wq.at[zat(k), core, pl.ds(pl.multiple_of(q * quarter, 16), quarter)]

    own_piece = wq_h.at[pl.ds(pl.multiple_of(x * quarter, 16), quarter)]
    query_ring = Ring(lambda k: query_piece(k, x), quarter // 2, wq_s, wq_r, zdev(1), zdev(-1), own_piece)

    def query_pass(k):
        dst = query_piece(k, x)
        for j in range(1, nx):
            remote(dst, dst, wq_xs.at[k % nz - 1, j - 1], wq_xr.at[k % nz - 1, j - 1], xdev(j))

    def query_wait(step):
        query_ring.wait(step, hz)
        if step < hz:
            query_ring.start(step + 1, hz)
        query_pass(step)
        if step < hz:
            query_pass(-step)

    def query_all():
        for k in range(1, nz):
            for j in range(1, nx):
                block = query_piece(k, xat(-j))
                remote(block, block, wq_xs.at[k - 1, j - 1], wq_xr.at[k - 1, j - 1], xdev(j), start=False).wait_recv()
        local[2].wait()
        remote(wq.at[:, core], wq.at[:, core], wq_cs, wq_cr, sib)

    def query_from_sibling():
        block = wq.at[:, 1 - core]
        remote(block, block, wq_cs, wq_cr, sib, start=False).wait_recv()

    with jax.named_scope("spread"):
        for k in sorted(range(1, ny), key=lambda k: -min(k, ny - k)):
            to = yat(k)
            remote(
                st_h.at[:, pl.ds(pl.multiple_of(to * piece, 16), piece), :],
                a2a.at[y], a2a_s.at[k - 1], a2a_r.at[k - 1], ydev(k),
            )
    with jax.named_scope("weights_0"):
        out_w.start()
        kv_w.start()
        query_ring.start(1, hz)
    with jax.named_scope("hidden_x"):
        local[4].wait()
        for b in range(cores * nz):
            ht[b // cores, b % cores] = hid[:, b * wide : (b + 1) * wide].T
        for j in range(1, nx):
            part_x = pl.ds(pl.multiple_of(xat(j) * quarter, 16), quarter)
            remote(ht.at[:, :, part_x], hx.at[x], hx_s.at[j - 1], hx_r.at[j - 1], xdev(j))
    with jax.named_scope("weights_1"):
        for step in (1, 2):
            out_w.wait(step)
            kv_w.wait(step)
            query_wait(step)

    chunks = 2
    share = tok // chunks

    def rs_move(chunk, way, step):
        lo, rows = chunk * share, share
        src = rs_out.at[way, step - 1, pl.ds(lo, rows)]
        if step == 1:
            rows = share // 2
            lo += way * rows
            src = gpart.at[hy, pl.ds(lo, rows)]
        dst = rs_in.at[way, step - 1, pl.ds(lo, rows)]
        return src, dst, rs_s.at[chunk, way, step - 1], rs_r.at[chunk, way, step - 1]

    def rs_start(chunk, step):
        for way, to in ((0, ydev(1)), (1, ydev(-1))):
            remote(*rs_move(chunk, way, step), to)

    def rs_wait(chunk, step):
        for way in range(2):
            _, dst, s, r = rs_move(chunk, way, step)
            remote(dst, dst, s, r, ydev(1), start=False).wait_recv()

    def rs_step(step):
        left = hy - step
        for chunk in range(chunks):
            rs_wait(chunk, step)
            for way, k in ((0, left), (1, ny - left)):
                lo, hi = chunk * share, (chunk + 1) * share
                if step == 1:
                    half = share // 2
                    other = lo + (1 - way) * half
                    rs_out[way, step, other : other + half] = gpart[k, other : other + half]
                    lo += way * half
                    hi = lo + half
                rs_out[way, step, lo:hi] = (
                    rs_in[way, step - 1, lo:hi].astype(F32) + gpart[k, lo:hi].astype(F32)
                ).astype(BF16)
            rs_start(chunk, step + 1)

    part_rows = pairs // chunks

    def pick_slot(chunk):
        return lambda k: picked.at[yat(k), pl.ds(chunk * part_rows, part_rows)]

    order = tuple(reversed(range(chunks)))
    pick_rings = {
        c: Ring(pick_slot(c), part_rows // 2, pick_s.at[c], pick_r.at[c], ydev(1), ydev(-1)) for c in order
    }

    def pick_start(step):
        for c in order:
            pick_rings[c].start(step, hy)

    def pick_wait(step):
        for c in order:
            pick_rings[c].wait(step, hy)
            if step < hy:
                pick_rings[c].start(step + 1, hy)

    with jax.named_scope("select"):
        for k in range(1, ny):
            block = a2a.at[yat(-k)]
            remote(block, block, a2a_s.at[k - 1], a2a_r.at[k - 1], ydev(k), start=False).wait_recv()
        local[0].wait()
        names = [owner[i % owner.shape[0], i // owner.shape[0]] for i in range(used)]
        for i in range(used):
            rank = sum([(names[i] == names[j]).astype(jnp.int32) for j in range(i)], jnp.int32(0))
            rank = jnp.minimum(rank, a2a.shape[1] - 1)
            picked[y, i * piece : (i + 1) * piece, :] = a2a[names[i], rank]
    with jax.named_scope("picked_0"):
        pick_start(1)
    with jax.named_scope("weights_2"):
        out_w.wait(3)
        out_w.wait(4)
        local[1].wait()
        out_w.from_sibling()
    with jax.named_scope("grad_partial"):
        local[3].wait()
        for k in range(ny):
            rows = rows_of(wo, yat(hy - k), proj)
            gpart[(hy - k) % ny] = dot(cot[...], rows[...], NT).astype(BF16)
    with jax.named_scope("rs_1"):
        for chunk in range(chunks):
            rs_start(chunk, 1)
    with jax.named_scope("picked_1"):
        pick_wait(1)
    with jax.named_scope("weights_3"):
        kv_w.wait(3)
        query_wait(3)
        kv_w.wait(4)
        query_wait(4)
        kv_w.from_sibling()
    with jax.named_scope("unpack"):
        for i in range(cores * nz):
            both = wkv[2 * kw_rows * i : 2 * kw_rows * (i + 1), :].astype(F32)
            kvw_f[kw_rows * i : kw_rows * (i + 1), :proj] = both[:kw_rows]
            kvw_f[kw_rows * i : kw_rows * (i + 1), proj:] = both[kw_rows:]
        kvw[...] = kvw_f[...].astype(BF16)

    per_span = pairs // spans

    def project(ks):
        for chunk in order:
            rows = slice(chunk * part_rows, (chunk + 1) * part_rows)
            made = dot(jnp.concatenate([picked[yat(k), rows, :] for k in ks], axis=0), kvw[...]).astype(BF16)
            for n, k in enumerate(ks):
                at = pl.ds(pl.multiple_of(yat(k) * per_span, 16), per_span)
                for u in range(spans // chunks):
                    lo = n * part_rows + u * per_span
                    kv[1 + chunk * (spans // chunks) + u, at, :] = made[lo : lo + per_span]
                if chunk == chunks - 1:
                    remote(kv.at[spans, at], kv.at[0, at], halo_s.at[k % ny], halo_r.at[k % ny], xdev(1))

    with jax.named_scope("project_1"):
        project((0, 1))
    with jax.named_scope("picked_2"):
        pick_wait(2)
    with jax.named_scope("rs_2"):
        rs_step(1)
    with jax.named_scope("project_2"):
        project((-1, 2))
    with jax.named_scope("picked_3"):
        pick_wait(3)
    with jax.named_scope("rs_3"):
        rs_step(2)
    with jax.named_scope("weights_5"):
        query_all()
        query_from_sibling()
    with jax.named_scope("queries"):
        qpad[pl.ds(1, tok), :] = dot(hid[...], wq[...].reshape(hid.shape[1], proj)).astype(BF16).astype(F32)
    with jax.named_scope("project_3"):
        project((-2, 3, -3))
    with jax.named_scope("picked_4"):
        pick_wait(4)
        project((4,))
    with jax.named_scope("rs_4"):
        rs_step(3)

    def forward(g):
        rows = pl.ds(g * span, span)
        for h in range(heads):
            cols = pl.ds(h * HEAD_DIM, HEAD_DIM)
            q = qpad[rows, cols].astype(BF16)
            scores = dot(q, kv[g, :, cols], NT) * scale
            e = jnp.exp(scores - jnp.max(scores, axis=-1, keepdims=True))
            p = e / jnp.sum(e, axis=-1, keepdims=True)
            probs[g * heads + h] = p
            out = dot(p.astype(BF16), kv[g, :, pl.ds(proj + h * HEAD_DIM, HEAD_DIM)])
            if g == 0:
                out = jnp.where(x == 0, jnp.zeros_like(out), out)
            apad[rows, cols] = out

    with jax.named_scope("forward"):
        for g in range(1, spans + 1):
            forward(g)
    with jax.named_scope("halo"):
        for k in range(ny):
            at = pl.ds(pl.multiple_of(yat(k) * per_span, 16), per_span)
            remote(kv.at[0, at], kv.at[0, at], halo_s.at[k], halo_r.at[k], xdev(1), start=False).wait_recv()
        forward(0)

    def att_slot(chunk):
        return lambda k: att.at[yat(k), pl.ds(chunk * share, share)]

    att_rings = [
        Ring(att_slot(c), share // 2, att_s.at[c], att_r.at[c], ydev(1), ydev(-1)) for c in range(chunks)
    ]

    def att_wait(step):
        for ring in att_rings:
            ring.wait(step, hy)
            if step < hy:
                ring.start(step + 1, hy)

    with jax.named_scope("att_1"):
        att[y] = apad[pl.ds(1, tok), :].astype(BF16)
        for ring in att_rings:
            ring.start(1, hy)
    with jax.named_scope("rs_last"):
        for chunk in range(chunks):
            rs_wait(chunk, hy)
        total = gpart[0].astype(F32) + rs_in[0, hy - 1].astype(F32) + rs_in[1, hy - 1].astype(F32)
        gpad[pl.ds(1, tok), :] = total.astype(BF16).astype(F32)

    def backward(g, h):
        rows = pl.ds(g * span, span)
        cols = pl.ds(h * HEAD_DIM, HEAD_DIM)
        p = probs[g * heads + h]
        gp = dot(gpad[rows, cols].astype(BF16), kv[g, :, pl.ds(proj + h * HEAD_DIM, HEAD_DIM)], NT)
        gs = (p * (gp - jnp.sum(p * gp, axis=-1, keepdims=True))).astype(BF16)
        out = dot(gs, kv[g, :, cols]) * scale
        if g == 0:
            out = jnp.where(x == 0, jnp.zeros_like(out), out)
        gqpad[rows, cols] = out

    def mix(k):
        rows = rows_of(wo, yat(k), proj)
        made = dot(att[yat(k)], rows[...])
        if k == 0:
            acc[...] = made
        else:
            acc[...] += made

    def gq_copy(h, j, start):
        block = gq.at[h, x] if start else gq.at[h, xat(-j)]
        return remote(block, block, gq_s.at[h, j - 1], gq_r.at[h, j - 1], xdev(j), start)

    with jax.named_scope("backward"):
        for h in range(heads):
            for g in range(spans + 1):
                backward(g, h)
            gq[h, x] = gqpad[pl.ds(1, tok), pl.ds(h * HEAD_DIM, HEAD_DIM)].astype(BF16)
            for j in range(1, nx):
                gq_copy(h, j, True)

    many = nz * cores * quarter

    with jax.named_scope("own_part"):
        mine = ht[:, :, pl.ds(pl.multiple_of(x * quarter, 16), quarter), :].reshape(many, tok)
        for h in range(heads):
            part[h] = dot(mine, gq[h, x]).reshape(nz, cores, quarter, HEAD_DIM)
        for j in range(1, nx):
            block = hx.at[xat(-j)]
            remote(block, block, hx_s.at[j - 1], hx_r.at[j - 1], xdev(j), start=False).wait_recv()

    def sib_copy(h, start):
        return remote(sib_out.at[h], sib_in.at[h], sib_s.at[h], sib_r.at[h], sib, start)

    def other_parts(h):
        for j in (1, nx - 1, *range(2, nx - 1)):
            gq_copy(h, j, False).wait_recv()
            place = xat(-j)
            part[h] += dot(hx[place].reshape(many, tok), gq[h, place]).reshape(nz, cores, quarter, HEAD_DIM)
        sib_out[h] = part[h, :, 1 - core].astype(BF16)
        sib_copy(h, True)

    def z_copy(h, p, start):
        return remote(zs.at[h, p], z_in.at[h, p], z_s.at[h, p], z_r.at[h, p], zdev(p + 1), start)

    def to_z(h):
        sib_copy(h, False).wait_recv()
        for p in range(nz):
            zs[h, p] = (part[h, zat(p + 1), core] + sib_in[h, zat(p + 1)].astype(F32)).astype(BF16)
            if p + 1 < nz:
                z_copy(h, p, True)

    def f_copy(h, j, start):
        block = fin.at[h, x] if start else fin.at[h, xat(-j)]
        return remote(block, block, f_s.at[h, j - 1], f_r.at[h, j - 1], xdev(j), start)

    def from_z(h):
        total = zs[h, nz - 1].astype(F32)
        for p in range(nz - 1):
            z_copy(h, p, False).wait_recv()
            total += z_in[h, p].astype(F32)
        fin[h, x] = total.astype(BF16)
        for j in range(1, nx):
            f_copy(h, j, True)

    with jax.named_scope("att_2"):
        att_wait(1)
    with jax.named_scope("part_0"):
        other_parts(0)
    with jax.named_scope("att_3"):
        att_wait(2)
    with jax.named_scope("to_z_0"):
        to_z(0)
    with jax.named_scope("part_1"):
        other_parts(1)
    with jax.named_scope("att_4"):
        att_wait(3)
    with jax.named_scope("to_z_1"):
        to_z(1)
    with jax.named_scope("mixed"):
        for k in (0, 1, -1, 2, -2, 3, -3):
            mix(k)
        att_wait(4)
        mix(4)
        mixed_o[...] = acc[...].astype(BF16)
    with jax.named_scope("from_z"):
        for h in range(heads):
            from_z(h)
    with jax.named_scope("from_x"):
        for h in range(heads):
            for j in range(1, nx):
                f_copy(h, j, False).wait_recv()
            grad_o[:, pl.ds(h * HEAD_DIM, HEAD_DIM)] = fin[h].astype(F32).reshape(wide, HEAD_DIM)
    with jax.named_scope("drain"):
        for copy in sent + [
            c for ring in (*out_w.rings, *kv_w.rings, query_ring, *pick_rings.values(), *att_rings) for c in ring.sent
        ]:
            copy.wait_send()


def shards(sizes, hidden, states, owner, query_w, key_w, value_w, out_w, cotangent):
    cores, nz, nx, ny = sizes
    tok, wide = hidden.shape
    slots, length, enc_d = states.shape
    spans, per = owner.shape
    proj = query_w.shape[1]
    heads = proj // HEAD_DIM
    n_dp = cores * nz
    used = spans * per
    piece = length // ny
    pairs = used * piece
    cols = out_w.shape[1]
    keys = per * length
    padded = tok + tok // spans
    dma = pltpu.SemaphoreType.DMA
    any_, vmem = pl.BlockSpec(memory_space=pltpu.HBM), pl.BlockSpec(memory_space=pltpu.VMEM)
    block = wide // n_dp
    quarter = block // nx
    scratch = [
        pltpu.VMEM((tok, wide), BF16),
        pltpu.VMEM((tok, cols), BF16),
        pltpu.VMEM(key_w.shape, BF16),
        pltpu.VMEM(key_w.shape, BF16),
        pltpu.VMEM((nz, cores, block, proj), BF16),
        pltpu.VMEM((n_dp * out_w.shape[0], cols), BF16),
        pltpu.VMEM((2 * enc_d, proj), BF16),
        pltpu.VMEM((enc_d, 2 * proj), F32),
        pltpu.VMEM((enc_d, 2 * proj), BF16),
        pltpu.VMEM((ny, slots, piece, enc_d), BF16),
        pltpu.VMEM((ny, pairs, enc_d), BF16),
        pltpu.VMEM((spans + 1, keys, 2 * proj), BF16),
        pltpu.VMEM((ny, tok, proj), BF16),
        pltpu.VMEM((2, ny // 2, tok, proj), BF16),
        pltpu.VMEM((2, ny // 2, tok, proj), BF16),
        pltpu.VMEM((padded, proj), F32),
        pltpu.VMEM((padded, proj), F32),
        pltpu.VMEM(((spans + 1) * heads, tok // spans, keys), F32),
        pltpu.VMEM((padded, proj), F32),
        pltpu.VMEM((ny, tok, proj), BF16),
        pltpu.VMEM((padded, proj), F32),
        pltpu.VMEM((nz, cores, block, tok), BF16),
        pltpu.VMEM((nx, nz, cores, quarter, tok), BF16),
        pltpu.VMEM((heads, nx, tok, HEAD_DIM), BF16),
        pltpu.VMEM((heads, nz, cores, quarter, HEAD_DIM), F32),
        pltpu.VMEM((heads, nz, quarter, HEAD_DIM), BF16),
        pltpu.VMEM((heads, nz, quarter, HEAD_DIM), BF16),
        pltpu.VMEM((heads, nz, quarter, HEAD_DIM), BF16),
        pltpu.VMEM((heads, nz - 1, quarter, HEAD_DIM), BF16),
        pltpu.VMEM((heads, nx, quarter, HEAD_DIM), BF16),
        pltpu.VMEM((tok, cols), F32),
        dma((7,)),
        dma((ny - 1,)), dma((ny - 1,)),
        dma((2, 2, ny // 2)), dma((2, 2, ny // 2)),
        dma((2, 2, ny // 2)), dma((2, 2, ny // 2)),
        dma((2, 2, ny // 2)), dma((2, 2, ny // 2)),
        dma((2, 2, nz // 2)), dma((2, 2, nz // 2)),
        dma((2, nz // 2)), dma((2, nz // 2)),
        dma((1, 2, nz // 2)), dma((1, 2, nz // 2)),
        dma((nz,)), dma((nz,)), dma(()), dma(()), dma((nz,)), dma((nz,)),
        dma((nz - 1, nx - 1)), dma((nz - 1, nx - 1)),
        dma((ny,)), dma((ny,)),
        dma((nx - 1,)), dma((nx - 1,)),
        dma((heads, nx - 1)), dma((heads, nx - 1)),
        dma((heads,)), dma((heads,)),
        dma((heads, nz - 1)), dma((heads, nz - 1)),
        dma((heads, nx - 1)), dma((heads, nx - 1)),
    ]
    operands = [
        pltpu.with_memory_space_constraint(a, pltpu.HBM)
        for a in (hidden, states, query_w, key_w, value_w, out_w, cotangent)
    ]
    operands.insert(2, owner.T)
    return pl.pallas_call(
        functools.partial(kernel, cores, nz, nx, ny, spans),
        out_shape=(
            jax.ShapeDtypeStruct((tok, cols), BF16),
            jax.ShapeDtypeStruct((wide // n_dp, proj), F32),
        ),
        in_specs=[any_, any_, pl.BlockSpec(memory_space=pltpu.SMEM), any_, any_, any_, any_, any_],
        out_specs=(vmem, vmem),
        scratch_shapes=scratch,
        compiler_params=pltpu.CompilerParams(
            collective_id=0, has_side_effects=True, vmem_limit_bytes=48 * 2**20
        ),
        cost_estimate=pl.CostEstimate(flops=3 * 10**9, bytes_accessed=8 * 2**20, transcendentals=163840),
    )(*operands)


def solution(mesh):
    sizes = (2, mesh.shape["dp"] // 2, mesh.shape["ctx"], mesh.shape["enc"])
    in_specs = (
        P(("dp", "ctx"), None),
        P(("dp", "ctx", "enc"), None, None),
        P(("dp", "ctx"), None),
        P("dp", "enc"),
        P("dp", "enc"),
        P("dp", "enc"),
        P("dp", "enc"),
        P(("dp", "ctx"), "enc"),
    )
    out_specs = (P(("dp", "ctx"), "enc"), P("dp", "enc"))
    return jax.shard_map(
        functools.partial(shards, sizes),
        mesh=mesh,
        in_specs=in_specs,
        out_specs=out_specs,
        check_vma=False,
    )
```

```python
import functools
import math

import jax
import jax.numpy as jnp
from jax import lax
from jax.experimental import pallas as pl
from jax.experimental.pallas import tpu as pltpu
from jax.sharding import PartitionSpec as P

HEAD_DIM = 128
MESH = pl.DeviceIdType.MESH
BF16 = jnp.bfloat16
F32 = jnp.float32
NT = (((1,), (1,)), ((), ()))


def dot(a, b, dims=(((1,), (0,)), ((), ()))):
    return lax.dot_general(a, b, dims, preferred_element_type=F32)


def rows_of(ref, index, count):
    step = 128 if count % 128 == 0 else 16
    return ref.at[pl.ds(pl.multiple_of(index * count, step), count)]


class Ring:
    def __init__(self, slot, first, send, recv, right, left, own=None, number=0):
        self.slot, self.number = slot, number
        self.first, self.send, self.recv = first, send, recv
        self.right, self.left, self.own = right, left, own
        self.sent = []

    def part(self, ref, half):
        if half == 0:
            return ref.at[pl.ds(0, self.first)]
        return ref.at[pl.ds(self.first, ref.shape[0] - self.first)]

    def start(self, step, last):
        for way, to, sign in ((0, self.right, -1), (1, self.left, 1)):
            dst = self.slot(sign * (step - 1))
            src = self.own if step == 1 and self.own is not None else dst
            if step == last:
                src, dst = self.part(src, way), self.part(dst, way)
            copy = pltpu.make_async_remote_copy(
                src_ref=src,
                dst_ref=dst,
                send_sem=self.send.at[way, step - 1],
                recv_sem=self.recv.at[way, step - 1],
                device_id=to,
                device_id_type=MESH,
            )
            copy.start()
            self.sent.append(copy)

    def wait(self, step, last):
        for way, sign in ((0, -1), (1, 1)):
            dst = self.slot(sign * step)
            if step == last:
                dst = self.part(dst, way)
            pltpu.make_async_remote_copy(
                src_ref=dst,
                dst_ref=dst,
                send_sem=self.send.at[way, step - 1],
                recv_sem=self.recv.at[way, step - 1],
                device_id=self.right,
                device_id_type=MESH,
            ).wait_recv()


def kernel(
    cores, nz, nx, ny, spans, hid_h, st_h, owner_h, wq_h, wk_h, wv_h, wo_h, cot_h, mixed_o, grad_o,
    owner, hid, cot, wk_v, wv_v, wq, wo, wkv, kvw_f, kvw, a2a_0, a2a_1, picked, kv, gpart, rs_out, rs_in, qpad, gpad, probs,
    apad, att, gqpad, ht, hx, gq, part, sib_out, sib_in, zs, z_in, fin, acc,
    local_sem, a2a_s, a2a_r, pick_s, pick_r, rs_s, rs_r, att_s, att_r,
    wo_s, wo_r, wq_s, wq_r, kw_s, kw_r, wo_cs, wo_cr, wq_cs, wq_cr, kw_cs, kw_cr, wq_xs, wq_xr,
    halo_s, halo_r, hx_s, hx_r, gq_s, gq_r, sib_s, sib_r, z_s, z_r, f_s, f_r,
):
    dp, x, y = lax.axis_index("dp"), lax.axis_index("ctx"), lax.axis_index("enc")
    z, core = lax.div(dp, cores), lax.rem(dp, cores)
    sib = {"dp": z * cores + (1 - core)}

    def zat(k):
        return lax.rem(z + (k + nz), nz)

    def xat(k):
        return lax.rem(x + (k + nx), nx)

    def yat(k):
        return lax.rem(y + (k + ny), ny)

    def zdev(k):
        return {"dp": zat(k) * cores + core}

    def xdev(k):
        return {"ctx": xat(k)}

    def ydev(k):
        return {"enc": yat(k)}

    hy, hz = ny // 2, nz // 2
    tok = hid.shape[0]
    proj = wq_h.shape[1]
    wide = wq_h.shape[0]
    quarter = wide // nx
    heads = proj // HEAD_DIM
    span = tok // spans
    pairs = picked.shape[1]
    used = owner.shape[0] * owner.shape[1]
    piece = pairs // used
    kw_rows = wk_v.shape[0]
    scale = 1.0 / math.sqrt(HEAD_DIM)
    sent = []

    def remote(src, dst, s, r, to, start=True):
        copy = pltpu.make_async_remote_copy(
            src_ref=src, dst_ref=dst, send_sem=s, recv_sem=r, device_id=to, device_id_type=MESH
        )
        if start:
            copy.start()
            sent.append(copy)
        return copy

    enc_d = st_h.shape[2]
    a2a = (a2a_0, a2a_1)
    lanes = (slice(0, a2a_0.shape[3]), slice(a2a_0.shape[3], enc_d))

    def lane(c):
        return pl.ds(lanes[c].start, lanes[c].stop - lanes[c].start)

    with jax.named_scope("entry"):
        barrier = pltpu.get_barrier_semaphore()
        peers = [sib]
        peers += [ydev(k) for k in range(1, ny)]
        peers += [xdev(k) for k in range(1, nx)]
        peers += [zdev(k) for k in range(1, nz)]
        for peer in peers:
            pl.semaphore_signal(barrier, inc=1, device_id=peer, device_id_type=MESH)

        local = [
            pltpu.make_async_copy(
                st_h.at[:, pl.ds(pl.multiple_of(y * piece, 16), piece), lane(0)], a2a_0.at[y], local_sem.at[0]
            ),
            pltpu.make_async_copy(wo_h, rows_of(wo, dp, wo_h.shape[0]), local_sem.at[1]),
            pltpu.make_async_copy(wq_h, wq.at[z, core], local_sem.at[2]),
            pltpu.make_async_copy(cot_h, cot, local_sem.at[3]),
            pltpu.make_async_copy(hid_h, hid, local_sem.at[4]),
            pltpu.make_async_copy(wk_h, wk_v, local_sem.at[5]),
            pltpu.make_async_copy(wv_h, wv_v, local_sem.at[6]),
            pltpu.make_async_copy(owner_h, owner, local_sem.at[7]),
            pltpu.make_async_copy(
                st_h.at[:, pl.ds(pl.multiple_of(y * piece, 16), piece), lane(1)], a2a_1.at[y], local_sem.at[8]
            ),
        ]
        for copy in local:
            copy.start()
        local[5].wait()
        local[6].wait()
        rows_of(wkv, dp, 2 * kw_rows)[...] = jnp.concatenate(
            [wk_v[...].astype(F32), wv_v[...].astype(F32)], axis=0
        ).astype(BF16)
        qpad[...] = jnp.zeros_like(qpad)
        gpad[...] = jnp.zeros_like(gpad)
        pl.semaphore_wait(barrier, len(peers))

    class Weight:
        def __init__(self, buf, own, cuts, s, r, to_sib, from_sib):
            self.rows = buf.shape[0] // (cores * nz)
            self.buf, self.own, self.s, self.r = buf, own, to_sib, from_sib
            self.rings = []
            for n, (lo, hi) in enumerate(zip(cuts, [*cuts[1:], self.rows])):
                part = pl.ds(lo, hi - lo)
                self.rings.append(
                    Ring(
                        lambda k, part=part: self.block(k, core).at[part],
                        (hi - lo + 16) // 32 * 16, s.at[n], r.at[n], zdev(1), zdev(-1),
                        None if own is None else own.at[part],
                    )
                )

        def block(self, k, c):
            return rows_of(self.buf, zat(k) * cores + c, self.rows)

        def start(self):
            for ring in self.rings:
                ring.start(1, hz)
            self.pass_on(0)

        def pass_on(self, k):
            block = self.block(k, core)
            src = self.own if k == 0 and self.own is not None else block
            remote(src, block, self.s.at[k % nz], self.r.at[k % nz], sib)

        def wait(self, step):
            for ring in self.rings:
                ring.wait(step, hz)
                if step < hz:
                    ring.start(step + 1, hz)
            self.pass_on(step)
            if step < hz:
                self.pass_on(-step)

        def from_sibling(self):
            for k in range(nz):
                block = self.block(k, 1 - core)
                remote(block, block, self.s.at[k], self.r.at[k], sib, start=False).wait_recv()

    out_w = Weight(wo, wo_h, (0, wo_h.shape[0] // 2), wo_s, wo_r, wo_cs, wo_cr)
    kv_w = Weight(wkv, None, (0,), kw_s, kw_r, kw_cs, kw_cr)

    def query_piece(k, q):
        return wq.at[zat(k), core, pl.ds(pl.multiple_of(q * quarter, 16), quarter)]

    own_piece = wq_h.at[pl.ds(pl.multiple_of(x * quarter, 16), quarter)]
    query_ring = Ring(lambda k: query_piece(k, x), quarter // 2, wq_s, wq_r, zdev(1), zdev(-1), own_piece)

    def query_pass(k):
        dst = query_piece(k, x)
        for j in range(1, nx):
            remote(dst, dst, wq_xs.at[k % nz - 1, j - 1], wq_xr.at[k % nz - 1, j - 1], xdev(j))

    def query_wait(step):
        query_ring.wait(step, hz)
        if step < hz:
            query_ring.start(step + 1, hz)
        query_pass(step)
        if step < hz:
            query_pass(-step)

    def query_all():
        for k in range(1, nz):
            for j in range(1, nx):
                block = query_piece(k, xat(-j))
                remote(block, block, wq_xs.at[k - 1, j - 1], wq_xr.at[k - 1, j - 1], xdev(j), start=False).wait_recv()
        local[2].wait()
        remote(wq.at[:, core], wq.at[:, core], wq_cs, wq_cr, sib)

    def query_from_sibling():
        block = wq.at[:, 1 - core]
        remote(block, block, wq_cs, wq_cr, sib, start=False).wait_recv()

    far_first = sorted(range(1, ny), key=lambda k: -min(k, ny - k))

    def spread(c):
        for k in far_first:
            to = pl.ds(pl.multiple_of(yat(k) * piece, 16), piece)
            remote(
                st_h.at[:, to, lane(c)], a2a[c].at[y], a2a_s.at[c, k - 1], a2a_r.at[c, k - 1], ydev(k)
            )

    with jax.named_scope("spread"):
        spread(0)
    with jax.named_scope("weights_0"):
        out_w.start()
        kv_w.start()
        query_ring.start(1, hz)
    with jax.named_scope("hidden_x"):
        local[4].wait()
        for b in range(cores * nz):
            ht[b // cores, b % cores] = hid[:, b * wide : (b + 1) * wide].T
        for j in range(1, nx):
            part_x = pl.ds(pl.multiple_of(xat(j) * quarter, 16), quarter)
            remote(ht.at[:, :, part_x], hx.at[x], hx_s.at[j - 1], hx_r.at[j - 1], xdev(j))
    with jax.named_scope("spread_1"):
        spread(1)

    def weights_step(step):
        out_w.wait(step)
        kv_w.wait(step)
        query_wait(step)

    with jax.named_scope("weights_1"):
        weights_step(1)

    chunks = 2
    share = tok // chunks

    half = tok // 2

    def rs_move(h, way, step):
        src, dst = rs_out.at[way, step - 1, h], rs_in.at[way, step - 1, h]
        if step == 1:
            rows = pl.ds(way * half, half)
            src, dst = gpart.at[hy, h, rows], dst.at[rows]
        return src, dst, rs_s.at[h, way, step - 1], rs_r.at[h, way, step - 1]

    def rs_start(h, step):
        for way, to in ((0, ydev(1)), (1, ydev(-1))):
            remote(*rs_move(h, way, step), to)

    def rs_wait(h, step):
        for way in range(2):
            _, dst, s, r = rs_move(h, way, step)
            remote(dst, dst, s, r, ydev(1), start=False).wait_recv()

    def rs_step(step):
        left = hy - step
        for h in range(heads):
            rs_wait(h, step)
            for way, k in ((0, left), (1, ny - left)):
                rows = slice(0, tok)
                if step == 1:
                    rows, other = slice(way * half, (way + 1) * half), slice((1 - way) * half, (2 - way) * half)
                    rs_out[way, step, h, other] = gpart[k, h, other]
                rs_out[way, step, h, rows] = (
                    rs_in[way, step - 1, h, rows].astype(F32) + gpart[k, h, rows].astype(F32)
                ).astype(BF16)
            rs_start(h, step + 1)

    def pick_slot(c):
        return lambda k: picked.at[yat(k), :, lane(c)]

    pick_rings = [Ring(pick_slot(c), pairs // 2, pick_s.at[c], pick_r.at[c], ydev(1), ydev(-1)) for c in range(2)]

    def pick_wait(c, step):
        pick_rings[c].wait(step, hy)
        if step < hy:
            pick_rings[c].start(step + 1, hy)

    def select(c):
        for k in range(1, ny):
            block = a2a[c].at[yat(-k)]
            remote(block, block, a2a_s.at[c, k - 1], a2a_r.at[c, k - 1], ydev(k), start=False).wait_recv()
        if c == 0:
            local[0].wait()
            local[7].wait()
        else:
            local[8].wait()
        names = [owner[i % owner.shape[0], i // owner.shape[0]] for i in range(used)]
        for i in range(used):
            rank = sum([(names[i] == names[j]).astype(jnp.int32) for j in range(i)], jnp.int32(0))
            rank = jnp.minimum(rank, a2a_0.shape[1] - 1)
            picked[y, i * piece : (i + 1) * piece, lanes[c]] = a2a[c][names[i], rank]

    with jax.named_scope("select"):
        select(0)
        pick_rings[0].start(1, hy)
    with jax.named_scope("weights_2"):
        weights_step(2)
    with jax.named_scope("picked_1"):
        pick_wait(0, 1)
    with jax.named_scope("select_1"):
        select(1)
        pick_rings[1].start(1, hy)
    with jax.named_scope("weights_3"):
        weights_step(3)
    with jax.named_scope("picked_2"):
        pick_wait(0, 2)
    with jax.named_scope("weights_4"):
        weights_step(4)
        local[1].wait()
        out_w.from_sibling()
    with jax.named_scope("grad_partial"):
        local[3].wait()
        for k in range(ny):
            rows = rows_of(wo, yat(hy - k), proj)
            made = dot(cot[...], rows[...], NT).astype(BF16)
            for h in range(heads):
                gpart[(hy - k) % ny, h] = made[:, h * HEAD_DIM : (h + 1) * HEAD_DIM]
    with jax.named_scope("rs_1"):
        for h in range(heads):
            rs_start(h, 1)
    with jax.named_scope("picked_3"):
        pick_wait(1, 1)
    with jax.named_scope("weights_5"):
        kv_w.from_sibling()
    with jax.named_scope("unpack"):
        for i in range(cores * nz):
            both = wkv[2 * kw_rows * i : 2 * kw_rows * (i + 1), :].astype(F32)
            kvw_f[kw_rows * i : kw_rows * (i + 1), :proj] = both[:kw_rows]
            kvw_f[kw_rows * i : kw_rows * (i + 1), proj:] = both[kw_rows:]
        kvw[...] = kvw_f[...].astype(BF16)

    per_span = pairs // spans

    def project(ks):
        made = dot(jnp.concatenate([picked[yat(k)] for k in ks], axis=0), kvw[...]).astype(BF16)
        for n, k in enumerate(ks):
            at = pl.ds(pl.multiple_of(yat(k) * per_span, 16), per_span)
            for u in range(spans):
                lo = n * pairs + u * per_span
                kv[1 + u, at, :] = made[lo : lo + per_span]
            remote(kv.at[spans, at], kv.at[0, at], halo_s.at[k % ny], halo_r.at[k % ny], xdev(1))

    with jax.named_scope("picked_4"):
        pick_wait(0, 3)
    with jax.named_scope("project_1"):
        project((0, 1, -1))
    with jax.named_scope("picked_5"):
        pick_wait(1, 2)
    with jax.named_scope("rs_2"):
        rs_step(1)
    with jax.named_scope("project_2"):
        project((2, -2))
    with jax.named_scope("weights_6"):
        query_all()
        query_from_sibling()
    with jax.named_scope("queries"):
        qpad[pl.ds(1, tok), :] = dot(hid[...], wq[...].reshape(hid.shape[1], proj)).astype(BF16).astype(F32)
    with jax.named_scope("picked_6"):
        pick_wait(0, 4)
        pick_wait(1, 3)
    with jax.named_scope("rs_3"):
        rs_step(2)
    with jax.named_scope("project_3"):
        project((3, -3))
    with jax.named_scope("picked_7"):
        pick_wait(1, 4)
        project((4,))
    with jax.named_scope("rs_4"):
        rs_step(3)

    def forward(g):
        rows = pl.ds(g * span, span)
        for h in range(heads):
            cols = pl.ds(h * HEAD_DIM, HEAD_DIM)
            q = qpad[rows, cols].astype(BF16)
            scores = dot(q, kv[g, :, cols], NT) * scale
            e = jnp.exp(scores - jnp.max(scores, axis=-1, keepdims=True))
            p = e / jnp.sum(e, axis=-1, keepdims=True)
            probs[g * heads + h] = p
            out = dot(p.astype(BF16), kv[g, :, pl.ds(proj + h * HEAD_DIM, HEAD_DIM)])
            if g == 0:
                out = jnp.where(x == 0, jnp.zeros_like(out), out)
            apad[rows, cols] = out

    with jax.named_scope("forward"):
        for g in range(1, spans + 1):
            forward(g)
    with jax.named_scope("halo"):
        for k in range(ny):
            at = pl.ds(pl.multiple_of(yat(k) * per_span, 16), per_span)
            remote(kv.at[0, at], kv.at[0, at], halo_s.at[k], halo_r.at[k], xdev(1), start=False).wait_recv()
        forward(0)

    def att_slot(chunk):
        return lambda k: att.at[yat(k), pl.ds(chunk * share, share)]

    att_rings = [
        Ring(att_slot(c), share // 2, att_s.at[c], att_r.at[c], ydev(1), ydev(-1)) for c in range(chunks)
    ]

    def att_wait(step):
        for ring in att_rings:
            ring.wait(step, hy)
            if step < hy:
                ring.start(step + 1, hy)

    with jax.named_scope("att_1"):
        att[y] = apad[pl.ds(1, tok), :].astype(BF16)
        for ring in att_rings:
            ring.start(1, hy)
    def backward(g, h):
        rows = pl.ds(g * span, span)
        cols = pl.ds(h * HEAD_DIM, HEAD_DIM)
        p = probs[g * heads + h]
        gp = dot(gpad[rows, cols].astype(BF16), kv[g, :, pl.ds(proj + h * HEAD_DIM, HEAD_DIM)], NT)
        gs = (p * (gp - jnp.sum(p * gp, axis=-1, keepdims=True))).astype(BF16)
        out = dot(gs, kv[g, :, cols]) * scale
        if g == 0:
            out = jnp.where(x == 0, jnp.zeros_like(out), out)
        gqpad[rows, cols] = out

    def mix(k):
        rows = rows_of(wo, yat(k), proj)
        made = dot(att[yat(k)], rows[...])
        if k == 0:
            acc[...] = made
        else:
            acc[...] += made

    def gq_copy(h, j, start):
        block = gq.at[h, x] if start else gq.at[h, xat(-j)]
        return remote(block, block, gq_s.at[h, j - 1], gq_r.at[h, j - 1], xdev(j), start)

    with jax.named_scope("backward"):
        for h in range(heads):
            rs_wait(h, hy)
            total = gpart[0, h].astype(F32) + rs_in[0, hy - 1, h].astype(F32) + rs_in[1, hy - 1, h].astype(F32)
            gpad[pl.ds(1, tok), pl.ds(h * HEAD_DIM, HEAD_DIM)] = total.astype(BF16).astype(F32)
            for g in range(spans + 1):
                backward(g, h)
            gq[h, x] = gqpad[pl.ds(1, tok), pl.ds(h * HEAD_DIM, HEAD_DIM)].astype(BF16)
            for j in range(1, nx):
                gq_copy(h, j, True)

    many = nz * cores * quarter

    with jax.named_scope("own_part"):
        mine = ht[:, :, pl.ds(pl.multiple_of(x * quarter, 16), quarter), :].reshape(many, tok)
        for h in range(heads):
            part[h] = dot(mine, gq[h, x]).reshape(nz, cores, quarter, HEAD_DIM)
        for j in range(1, nx):
            block = hx.at[xat(-j)]
            remote(block, block, hx_s.at[j - 1], hx_r.at[j - 1], xdev(j), start=False).wait_recv()

    def sib_copy(h, start):
        return remote(sib_out.at[h], sib_in.at[h], sib_s.at[h], sib_r.at[h], sib, start)

    def other_parts(h):
        for j in (1, nx - 1, *range(2, nx - 1)):
            gq_copy(h, j, False).wait_recv()
            place = xat(-j)
            part[h] += dot(hx[place].reshape(many, tok), gq[h, place]).reshape(nz, cores, quarter, HEAD_DIM)
        sib_out[h] = part[h, :, 1 - core].astype(BF16)
        sib_copy(h, True)

    def z_copy(h, p, start):
        return remote(zs.at[h, p], z_in.at[h, p], z_s.at[h, p], z_r.at[h, p], zdev(p + 1), start)

    def to_z(h):
        sib_copy(h, False).wait_recv()
        for p in range(nz):
            zs[h, p] = (part[h, zat(p + 1), core] + sib_in[h, zat(p + 1)].astype(F32)).astype(BF16)
            if p + 1 < nz:
                z_copy(h, p, True)

    def f_copy(h, j, start):
        block = fin.at[h, x] if start else fin.at[h, xat(-j)]
        return remote(block, block, f_s.at[h, j - 1], f_r.at[h, j - 1], xdev(j), start)

    def from_z(h):
        total = zs[h, nz - 1].astype(F32)
        for p in range(nz - 1):
            z_copy(h, p, False).wait_recv()
            total += z_in[h, p].astype(F32)
        fin[h, x] = total.astype(BF16)
        for j in range(1, nx):
            f_copy(h, j, True)

    with jax.named_scope("att_2"):
        att_wait(1)
    with jax.named_scope("part_0"):
        other_parts(0)
    with jax.named_scope("att_3"):
        att_wait(2)
    with jax.named_scope("to_z_0"):
        to_z(0)
    with jax.named_scope("part_1"):
        other_parts(1)
    with jax.named_scope("att_4"):
        att_wait(3)
    with jax.named_scope("to_z_1"):
        to_z(1)
    with jax.named_scope("mixed"):
        for k in (0, 1, -1, 2, -2, 3, -3):
            mix(k)
        att_wait(4)
        mix(4)
        mixed_o[...] = acc[...].astype(BF16)
    with jax.named_scope("from_z"):
        for h in range(heads):
            from_z(h)
    with jax.named_scope("from_x"):
        for h in range(heads):
            for j in range(1, nx):
                f_copy(h, j, False).wait_recv()
            grad_o[:, pl.ds(h * HEAD_DIM, HEAD_DIM)] = fin[h].astype(F32).reshape(wide, HEAD_DIM)
    with jax.named_scope("drain"):
        for copy in sent + [
            c for ring in (*out_w.rings, *kv_w.rings, query_ring, *pick_rings, *att_rings) for c in ring.sent
        ]:
            copy.wait_send()


def shards(sizes, hidden, states, owner, query_w, key_w, value_w, out_w, cotangent):
    cores, nz, nx, ny = sizes
    tok, wide = hidden.shape
    slots, length, enc_d = states.shape
    spans, per = owner.shape
    proj = query_w.shape[1]
    heads = proj // HEAD_DIM
    n_dp = cores * nz
    used = spans * per
    piece = length // ny
    pairs = used * piece
    cols = out_w.shape[1]
    keys = per * length
    padded = tok + tok // spans
    dma = pltpu.SemaphoreType.DMA
    any_, vmem = pl.BlockSpec(memory_space=pltpu.HBM), pl.BlockSpec(memory_space=pltpu.VMEM)
    block = wide // n_dp
    quarter = block // nx
    scratch = [
        pltpu.SMEM((per, spans), jnp.int32),
        pltpu.VMEM((tok, wide), BF16),
        pltpu.VMEM((tok, cols), BF16),
        pltpu.VMEM(key_w.shape, BF16),
        pltpu.VMEM(key_w.shape, BF16),
        pltpu.VMEM((nz, cores, block, proj), BF16),
        pltpu.VMEM((n_dp * out_w.shape[0], cols), BF16),
        pltpu.VMEM((2 * enc_d, proj), BF16),
        pltpu.VMEM((enc_d, 2 * proj), F32),
        pltpu.VMEM((enc_d, 2 * proj), BF16),
        pltpu.VMEM((ny, slots, piece, enc_d // 256 * 128 + 128), BF16),
        pltpu.VMEM((ny, slots, piece, enc_d - enc_d // 256 * 128 - 128), BF16),
        pltpu.VMEM((ny, pairs, enc_d), BF16),
        pltpu.VMEM((spans + 1, keys, 2 * proj), BF16),
        pltpu.VMEM((ny, heads, tok, HEAD_DIM), BF16),
        pltpu.VMEM((2, ny // 2, heads, tok, HEAD_DIM), BF16),
        pltpu.VMEM((2, ny // 2, heads, tok, HEAD_DIM), BF16),
        pltpu.VMEM((padded, proj), F32),
        pltpu.VMEM((padded, proj), F32),
        pltpu.VMEM(((spans + 1) * heads, tok // spans, keys), F32),
        pltpu.VMEM((padded, proj), F32),
        pltpu.VMEM((ny, tok, proj), BF16),
        pltpu.VMEM((padded, proj), F32),
        pltpu.VMEM((nz, cores, block, tok), BF16),
        pltpu.VMEM((nx, nz, cores, quarter, tok), BF16),
        pltpu.VMEM((heads, nx, tok, HEAD_DIM), BF16),
        pltpu.VMEM((heads, nz, cores, quarter, HEAD_DIM), F32),
        pltpu.VMEM((heads, nz, quarter, HEAD_DIM), BF16),
        pltpu.VMEM((heads, nz, quarter, HEAD_DIM), BF16),
        pltpu.VMEM((heads, nz, quarter, HEAD_DIM), BF16),
        pltpu.VMEM((heads, nz - 1, quarter, HEAD_DIM), BF16),
        pltpu.VMEM((heads, nx, quarter, HEAD_DIM), BF16),
        pltpu.VMEM((tok, cols), F32),
        dma((9,)),
        dma((2, ny - 1)), dma((2, ny - 1)),
        dma((2, 2, ny // 2)), dma((2, 2, ny // 2)),
        dma((2, 2, ny // 2)), dma((2, 2, ny // 2)),
        dma((2, 2, ny // 2)), dma((2, 2, ny // 2)),
        dma((2, 2, nz // 2)), dma((2, 2, nz // 2)),
        dma((2, nz // 2)), dma((2, nz // 2)),
        dma((1, 2, nz // 2)), dma((1, 2, nz // 2)),
        dma((nz,)), dma((nz,)), dma(()), dma(()), dma((nz,)), dma((nz,)),
        dma((nz - 1, nx - 1)), dma((nz - 1, nx - 1)),
        dma((ny,)), dma((ny,)),
        dma((nx - 1,)), dma((nx - 1,)),
        dma((heads, nx - 1)), dma((heads, nx - 1)),
        dma((heads,)), dma((heads,)),
        dma((heads, nz - 1)), dma((heads, nz - 1)),
        dma((heads, nx - 1)), dma((heads, nx - 1)),
    ]
    operands = [
        pltpu.with_memory_space_constraint(a, pltpu.HBM)
        for a in (hidden, states, owner.T, query_w, key_w, value_w, out_w, cotangent)
    ]
    return pl.pallas_call(
        functools.partial(kernel, cores, nz, nx, ny, spans),
        out_shape=(
            jax.ShapeDtypeStruct((tok, cols), BF16),
            jax.ShapeDtypeStruct((wide // n_dp, proj), F32),
        ),
        in_specs=[any_, any_, any_, any_, any_, any_, any_, any_],
        out_specs=(vmem, vmem),
        scratch_shapes=scratch,
        compiler_params=pltpu.CompilerParams(
            collective_id=0, has_side_effects=True, vmem_limit_bytes=48 * 2**20
        ),
        cost_estimate=pl.CostEstimate(flops=3 * 10**9, bytes_accessed=8 * 2**20, transcendentals=163840),
    )(*operands)


def solution(mesh):
    sizes = (2, mesh.shape["dp"] // 2, mesh.shape["ctx"], mesh.shape["enc"])
    in_specs = (
        P(("dp", "ctx"), None),
        P(("dp", "ctx", "enc"), None, None),
        P(("dp", "ctx"), None),
        P("dp", "enc"),
        P("dp", "enc"),
        P("dp", "enc"),
        P("dp", "enc"),
        P(("dp", "ctx"), "enc"),
    )
    out_specs = (P(("dp", "ctx"), "enc"), P("dp", "enc"))
    return jax.shard_map(
        functools.partial(shards, sizes),
        mesh=mesh,
        in_specs=in_specs,
        out_specs=out_specs,
        check_vma=False,
    )
```

```python
import functools
import math

import jax
import jax.numpy as jnp
from jax import lax
from jax.experimental import pallas as pl
from jax.experimental.pallas import tpu as pltpu
from jax.sharding import PartitionSpec as P

HEAD_DIM = 128
MESH = pl.DeviceIdType.MESH
BF16 = jnp.bfloat16
F32 = jnp.float32
NT = (((1,), (1,)), ((), ()))


def dot(a, b, dims=(((1,), (0,)), ((), ()))):
    return lax.dot_general(a, b, dims, preferred_element_type=F32)


def rows_of(ref, index, count):
    step = 128 if count % 128 == 0 else 16
    return ref.at[pl.ds(pl.multiple_of(index * count, step), count)]


class Ring:
    def __init__(self, slot, first, send, recv, right, left, own=None, number=0):
        self.slot, self.number = slot, number
        self.first, self.send, self.recv = first, send, recv
        self.right, self.left, self.own = right, left, own
        self.sent = []

    def part(self, ref, half):
        if half == 0:
            return ref.at[pl.ds(0, self.first)]
        return ref.at[pl.ds(self.first, ref.shape[0] - self.first)]

    def start(self, step, last):
        for way, to, sign in ((0, self.right, -1), (1, self.left, 1)):
            dst = self.slot(sign * (step - 1))
            src = self.own if step == 1 and self.own is not None else dst
            if step == last:
                src, dst = self.part(src, way), self.part(dst, way)
            copy = pltpu.make_async_remote_copy(
                src_ref=src,
                dst_ref=dst,
                send_sem=self.send.at[way, step - 1],
                recv_sem=self.recv.at[way, step - 1],
                device_id=to,
                device_id_type=MESH,
            )
            copy.start()
            self.sent.append(copy)

    def wait(self, step, last):
        for way, sign in ((0, -1), (1, 1)):
            dst = self.slot(sign * step)
            if step == last:
                dst = self.part(dst, way)
            pltpu.make_async_remote_copy(
                src_ref=dst,
                dst_ref=dst,
                send_sem=self.send.at[way, step - 1],
                recv_sem=self.recv.at[way, step - 1],
                device_id=self.right,
                device_id_type=MESH,
            ).wait_recv()


def kernel(
    cores, nz, nx, ny, spans, hid_h, st_h, owner_h, wq_h, wk_h, wv_h, wo_h, cot_h, mixed_o, grad_o,
    owner, hid, cot, wk_v, wv_v, wq, wo, wkv, kvw_f, kvw, a2a_0, a2a_1, picked, kv, gpart, rs_out, rs_in, qpad, gpad, probs,
    apad, att, gqpad, ht, hx, gq, part, sib_out, sib_in, zs, z_in, fin, acc,
    local_sem, a2a_s, a2a_r, pick_s, pick_r, rs_s, rs_r, att_s, att_r,
    wo_s, wo_r, wq_s, wq_r, kw_s, kw_r, wo_cs, wo_cr, wq_cs, wq_cr, kw_cs, kw_cr, wq_xs, wq_xr,
    halo_s, halo_r, hx_s, hx_r, gq_s, gq_r, sib_s, sib_r, z_s, z_r, f_s, f_r,
):
    dp, x, y = lax.axis_index("dp"), lax.axis_index("ctx"), lax.axis_index("enc")
    z, core = lax.div(dp, cores), lax.rem(dp, cores)
    sib = {"dp": z * cores + (1 - core)}

    def zat(k):
        return lax.rem(z + (k + nz), nz)

    def xat(k):
        return lax.rem(x + (k + nx), nx)

    def yat(k):
        return lax.rem(y + (k + ny), ny)

    def zdev(k):
        return {"dp": zat(k) * cores + core}

    def xdev(k):
        return {"ctx": xat(k)}

    def ydev(k):
        return {"enc": yat(k)}

    hy, hz = ny // 2, nz // 2
    tok = hid.shape[0]
    proj = wq_h.shape[1]
    wide = wq_h.shape[0]
    quarter = wide // nx
    heads = proj // HEAD_DIM
    span = tok // spans
    pairs = picked.shape[1]
    used = owner.shape[0] * owner.shape[1]
    piece = pairs // used
    kw_rows = wk_v.shape[0]
    scale = 1.0 / math.sqrt(HEAD_DIM)
    sent = []

    def remote(src, dst, s, r, to, start=True):
        copy = pltpu.make_async_remote_copy(
            src_ref=src, dst_ref=dst, send_sem=s, recv_sem=r, device_id=to, device_id_type=MESH
        )
        if start:
            copy.start()
            sent.append(copy)
        return copy

    enc_d = st_h.shape[2]
    a2a = (a2a_0, a2a_1)
    lanes = (slice(0, a2a_0.shape[3]), slice(a2a_0.shape[3], enc_d))

    def lane(c):
        return pl.ds(lanes[c].start, lanes[c].stop - lanes[c].start)

    with jax.named_scope("entry"):
        barrier = pltpu.get_barrier_semaphore()
        peers = [sib]
        peers += [ydev(k) for k in range(1, ny)]
        peers += [xdev(k) for k in range(1, nx)]
        peers += [zdev(k) for k in range(1, nz)]
        for peer in peers:
            pl.semaphore_signal(barrier, inc=1, device_id=peer, device_id_type=MESH)

        local = [
            pltpu.make_async_copy(
                st_h.at[:, pl.ds(pl.multiple_of(y * piece, 16), piece), lane(0)], a2a_0.at[y], local_sem.at[0]
            ),
            pltpu.make_async_copy(wo_h, rows_of(wo, dp, wo_h.shape[0]), local_sem.at[1]),
            pltpu.make_async_copy(wq_h, wq.at[z, core], local_sem.at[2]),
            pltpu.make_async_copy(cot_h, cot, local_sem.at[3]),
            pltpu.make_async_copy(hid_h, hid, local_sem.at[4]),
            pltpu.make_async_copy(wk_h, wk_v, local_sem.at[5]),
            pltpu.make_async_copy(wv_h, wv_v, local_sem.at[6]),
            pltpu.make_async_copy(owner_h, owner, local_sem.at[7]),
            pltpu.make_async_copy(
                st_h.at[:, pl.ds(pl.multiple_of(y * piece, 16), piece), lane(1)], a2a_1.at[y], local_sem.at[8]
            ),
        ]
        for copy in local:
            copy.start()
        local[5].wait()
        local[6].wait()
        rows_of(wkv, dp, 2 * kw_rows)[...] = jnp.concatenate(
            [wk_v[...].astype(F32), wv_v[...].astype(F32)], axis=0
        ).astype(BF16)
        qpad[...] = jnp.zeros_like(qpad)
        gpad[...] = jnp.zeros_like(gpad)
        pl.semaphore_wait(barrier, len(peers))

    class Weight:
        def __init__(self, buf, own, cuts, s, r, to_sib, from_sib):
            self.rows = buf.shape[0] // (cores * nz)
            self.buf, self.own, self.s, self.r = buf, own, to_sib, from_sib
            self.rings = []
            for n, (lo, hi) in enumerate(zip(cuts, [*cuts[1:], self.rows])):
                part = pl.ds(lo, hi - lo)
                self.rings.append(
                    Ring(
                        lambda k, part=part: self.block(k, core).at[part],
                        (hi - lo + 16) // 32 * 16, s.at[n], r.at[n], zdev(1), zdev(-1),
                        None if own is None else own.at[part],
                    )
                )

        def block(self, k, c):
            return rows_of(self.buf, zat(k) * cores + c, self.rows)

        def start(self):
            for ring in self.rings:
                ring.start(1, hz)
            self.pass_on(0)

        def pass_on(self, k):
            block = self.block(k, core)
            src = self.own if k == 0 and self.own is not None else block
            remote(src, block, self.s.at[k % nz], self.r.at[k % nz], sib)

        def wait(self, step):
            for ring in self.rings:
                ring.wait(step, hz)
                if step < hz:
                    ring.start(step + 1, hz)
            self.pass_on(step)
            if step < hz:
                self.pass_on(-step)

        def from_sibling(self):
            for k in range(nz):
                block = self.block(k, 1 - core)
                remote(block, block, self.s.at[k], self.r.at[k], sib, start=False).wait_recv()

    out_w = Weight(wo, wo_h, (0, wo_h.shape[0] // 2), wo_s, wo_r, wo_cs, wo_cr)
    kv_w = Weight(wkv, None, (0,), kw_s, kw_r, kw_cs, kw_cr)

    def query_piece(k, q):
        return wq.at[zat(k), core, pl.ds(pl.multiple_of(q * quarter, 16), quarter)]

    own_piece = wq_h.at[pl.ds(pl.multiple_of(x * quarter, 16), quarter)]
    query_ring = Ring(lambda k: query_piece(k, x), quarter // 2, wq_s, wq_r, zdev(1), zdev(-1), own_piece)

    def query_pass(k):
        dst = query_piece(k, x)
        for j in range(1, nx):
            remote(dst, dst, wq_xs.at[k % nz - 1, j - 1], wq_xr.at[k % nz - 1, j - 1], xdev(j))

    def query_wait(step):
        query_ring.wait(step, hz)
        if step < hz:
            query_ring.start(step + 1, hz)
        query_pass(step)
        if step < hz:
            query_pass(-step)

    def query_all():
        for k in range(1, nz):
            for j in range(1, nx):
                block = query_piece(k, xat(-j))
                remote(block, block, wq_xs.at[k - 1, j - 1], wq_xr.at[k - 1, j - 1], xdev(j), start=False).wait_recv()
        local[2].wait()
        remote(wq.at[:, core], wq.at[:, core], wq_cs, wq_cr, sib)

    def query_from_sibling():
        block = wq.at[:, 1 - core]
        remote(block, block, wq_cs, wq_cr, sib, start=False).wait_recv()

    far_first = sorted(range(1, ny), key=lambda k: -min(k, ny - k))

    def spread(c):
        for k in far_first:
            to = pl.ds(pl.multiple_of(yat(k) * piece, 16), piece)
            remote(
                st_h.at[:, to, lane(c)], a2a[c].at[y], a2a_s.at[c, k - 1], a2a_r.at[c, k - 1], ydev(k)
            )

    with jax.named_scope("spread"):
        spread(0)
    with jax.named_scope("weights_0"):
        out_w.start()
        kv_w.start()
        query_ring.start(1, hz)
    with jax.named_scope("hidden_x"):
        local[4].wait()
        for b in range(cores * nz):
            ht[b // cores, b % cores] = hid[:, b * wide : (b + 1) * wide].T
        for j in range(1, nx):
            part_x = pl.ds(pl.multiple_of(xat(j) * quarter, 16), quarter)
            remote(ht.at[:, :, part_x], hx.at[x], hx_s.at[j - 1], hx_r.at[j - 1], xdev(j))
    with jax.named_scope("spread_1"):
        spread(1)

    def weights_step(step):
        out_w.wait(step)
        kv_w.wait(step)
        query_wait(step)

    with jax.named_scope("weights_1"):
        weights_step(1)

    chunks = 2
    share = tok // chunks

    half = tok // 2

    def rs_move(h, way, step):
        src, dst = rs_out.at[way, step - 1, h], rs_in.at[way, step - 1, h]
        if step == 1:
            rows = pl.ds(way * half, half)
            src, dst = gpart.at[hy, h, rows], dst.at[rows]
        return src, dst, rs_s.at[h, way, step - 1], rs_r.at[h, way, step - 1]

    def rs_start(h, step):
        for way, to in ((0, ydev(1)), (1, ydev(-1))):
            remote(*rs_move(h, way, step), to)

    def rs_wait(h, step):
        for way in range(2):
            _, dst, s, r = rs_move(h, way, step)
            remote(dst, dst, s, r, ydev(1), start=False).wait_recv()

    def rs_step(step):
        left = hy - step
        for h in range(heads):
            rs_wait(h, step)
            for way, k in ((0, left), (1, ny - left)):
                rows = slice(0, tok)
                if step == 1:
                    rows, other = slice(way * half, (way + 1) * half), slice((1 - way) * half, (2 - way) * half)
                    rs_out[way, step, h, other] = gpart[k, h, other]
                rs_out[way, step, h, rows] = (
                    rs_in[way, step - 1, h, rows].astype(F32) + gpart[k, h, rows].astype(F32)
                ).astype(BF16)
            rs_start(h, step + 1)

    def pick_slot(c):
        return lambda k: picked.at[yat(k), :, lane(c)]

    pick_rings = [Ring(pick_slot(c), pairs // 2, pick_s.at[c], pick_r.at[c], ydev(1), ydev(-1)) for c in range(2)]

    def pick_wait(c, step):
        pick_rings[c].wait(step, hy)
        if step < hy:
            pick_rings[c].start(step + 1, hy)

    def select(c):
        for k in range(1, ny):
            block = a2a[c].at[yat(-k)]
            remote(block, block, a2a_s.at[c, k - 1], a2a_r.at[c, k - 1], ydev(k), start=False).wait_recv()
        if c == 0:
            local[0].wait()
            local[7].wait()
        else:
            local[8].wait()
        names = [owner[i % owner.shape[0], i // owner.shape[0]] for i in range(used)]
        for i in range(used):
            rank = sum([(names[i] == names[j]).astype(jnp.int32) for j in range(i)], jnp.int32(0))
            rank = jnp.minimum(rank, a2a_0.shape[1] - 1)
            picked[y, i * piece : (i + 1) * piece, lanes[c]] = a2a[c][names[i], rank]

    with jax.named_scope("select"):
        select(0)
        pick_rings[0].start(1, hy)
    with jax.named_scope("weights_2"):
        weights_step(2)
    with jax.named_scope("picked_1"):
        pick_wait(0, 1)
    with jax.named_scope("select_1"):
        select(1)
        pick_rings[1].start(1, hy)
    with jax.named_scope("weights_3"):
        weights_step(3)
    with jax.named_scope("picked_2"):
        pick_wait(0, 2)
    with jax.named_scope("weights_4"):
        weights_step(4)
        local[1].wait()
        out_w.from_sibling()
    with jax.named_scope("grad_partial"):
        local[3].wait()
        for k in range(ny):
            rows = rows_of(wo, yat(hy - k), proj)
            made = dot(cot[...], rows[...], NT).astype(BF16)
            for h in range(heads):
                gpart[(hy - k) % ny, h] = made[:, h * HEAD_DIM : (h + 1) * HEAD_DIM]
    with jax.named_scope("rs_1"):
        for h in range(heads):
            rs_start(h, 1)
    with jax.named_scope("picked_3"):
        pick_wait(1, 1)
    with jax.named_scope("weights_5"):
        kv_w.from_sibling()
    with jax.named_scope("unpack"):
        for i in range(cores * nz):
            both = wkv[2 * kw_rows * i : 2 * kw_rows * (i + 1), :].astype(F32)
            kvw_f[kw_rows * i : kw_rows * (i + 1), :proj] = both[:kw_rows]
            kvw_f[kw_rows * i : kw_rows * (i + 1), proj:] = both[kw_rows:]
        kvw[...] = kvw_f[...].astype(BF16)

    per_span = pairs // spans

    def project(ks):
        made = dot(jnp.concatenate([picked[yat(k)] for k in ks], axis=0), kvw[...]).astype(BF16)
        for n, k in enumerate(ks):
            at = pl.ds(pl.multiple_of(yat(k) * per_span, 16), per_span)
            for u in range(spans):
                lo = n * pairs + u * per_span
                kv[1 + u, at, :] = made[lo : lo + per_span]
            remote(kv.at[spans, at], kv.at[0, at], halo_s.at[k % ny], halo_r.at[k % ny], xdev(1))

    with jax.named_scope("rs_2"):
        rs_step(1)
    with jax.named_scope("picked_4"):
        pick_wait(0, 3)
    with jax.named_scope("project_1"):
        project((0, 1, -1))
    with jax.named_scope("picked_5"):
        pick_wait(1, 2)
    with jax.named_scope("project_2"):
        project((2, -2))
    with jax.named_scope("rs_3"):
        rs_step(2)
    with jax.named_scope("weights_6"):
        query_all()
        query_from_sibling()
    with jax.named_scope("queries"):
        qpad[pl.ds(1, tok), :] = dot(hid[...], wq[...].reshape(hid.shape[1], proj)).astype(BF16).astype(F32)
    with jax.named_scope("picked_6"):
        pick_wait(0, 4)
        pick_wait(1, 3)
    with jax.named_scope("project_3"):
        project((3, -3))
    with jax.named_scope("picked_7"):
        pick_wait(1, 4)
        project((4,))
    with jax.named_scope("rs_4"):
        rs_step(3)

    def forward(g):
        rows = pl.ds(g * span, span)
        for h in range(heads):
            cols = pl.ds(h * HEAD_DIM, HEAD_DIM)
            q = qpad[rows, cols].astype(BF16)
            scores = dot(q, kv[g, :, cols], NT) * scale
            e = jnp.exp(scores - jnp.max(scores, axis=-1, keepdims=True))
            p = e / jnp.sum(e, axis=-1, keepdims=True)
            probs[g * heads + h] = p
            out = dot(p.astype(BF16), kv[g, :, pl.ds(proj + h * HEAD_DIM, HEAD_DIM)])
            if g == 0:
                out = jnp.where(x == 0, jnp.zeros_like(out), out)
            apad[rows, cols] = out

    with jax.named_scope("forward"):
        for g in range(1, spans + 1):
            forward(g)
    with jax.named_scope("halo"):
        for k in range(ny):
            at = pl.ds(pl.multiple_of(yat(k) * per_span, 16), per_span)
            remote(kv.at[0, at], kv.at[0, at], halo_s.at[k], halo_r.at[k], xdev(1), start=False).wait_recv()
        forward(0)

    def att_slot(chunk):
        return lambda k: att.at[yat(k), pl.ds(chunk * share, share)]

    att_rings = [
        Ring(att_slot(c), share // 2, att_s.at[c], att_r.at[c], ydev(1), ydev(-1)) for c in range(chunks)
    ]

    def att_wait(step):
        for ring in att_rings:
            ring.wait(step, hy)
            if step < hy:
                ring.start(step + 1, hy)

    with jax.named_scope("att_1"):
        att[y] = apad[pl.ds(1, tok), :].astype(BF16)
        for ring in att_rings:
            ring.start(1, hy)
    def backward(g, h):
        rows = pl.ds(g * span, span)
        cols = pl.ds(h * HEAD_DIM, HEAD_DIM)
        p = probs[g * heads + h]
        gp = dot(gpad[rows, cols].astype(BF16), kv[g, :, pl.ds(proj + h * HEAD_DIM, HEAD_DIM)], NT)
        gs = (p * (gp - jnp.sum(p * gp, axis=-1, keepdims=True))).astype(BF16)
        out = dot(gs, kv[g, :, cols]) * scale
        if g == 0:
            out = jnp.where(x == 0, jnp.zeros_like(out), out)
        gqpad[rows, cols] = out

    def mix(k):
        rows = rows_of(wo, yat(k), proj)
        made = dot(att[yat(k)], rows[...])
        if k == 0:
            acc[...] = made
        else:
            acc[...] += made

    def gq_copy(h, j, start):
        block = gq.at[h, x] if start else gq.at[h, xat(-j)]
        return remote(block, block, gq_s.at[h, j - 1], gq_r.at[h, j - 1], xdev(j), start)

    with jax.named_scope("backward"):
        for h in range(heads):
            rs_wait(h, hy)
            total = gpart[0, h].astype(F32) + rs_in[0, hy - 1, h].astype(F32) + rs_in[1, hy - 1, h].astype(F32)
            gpad[pl.ds(1, tok), pl.ds(h * HEAD_DIM, HEAD_DIM)] = total.astype(BF16).astype(F32)
            for g in range(spans + 1):
                backward(g, h)
            gq[h, x] = gqpad[pl.ds(1, tok), pl.ds(h * HEAD_DIM, HEAD_DIM)].astype(BF16)
            for j in range(1, nx):
                gq_copy(h, j, True)

    many = nz * cores * quarter

    with jax.named_scope("own_part"):
        mine = ht[:, :, pl.ds(pl.multiple_of(x * quarter, 16), quarter), :].reshape(many, tok)
        for h in range(heads):
            part[h] = dot(mine, gq[h, x]).reshape(nz, cores, quarter, HEAD_DIM)
        for j in range(1, nx):
            block = hx.at[xat(-j)]
            remote(block, block, hx_s.at[j - 1], hx_r.at[j - 1], xdev(j), start=False).wait_recv()

    def sib_copy(h, start):
        return remote(sib_out.at[h], sib_in.at[h], sib_s.at[h], sib_r.at[h], sib, start)

    def other_parts(h):
        for j in (1, nx - 1, *range(2, nx - 1)):
            gq_copy(h, j, False).wait_recv()
            place = xat(-j)
            part[h] += dot(hx[place].reshape(many, tok), gq[h, place]).reshape(nz, cores, quarter, HEAD_DIM)
        sib_out[h] = part[h, :, 1 - core].astype(BF16)
        sib_copy(h, True)

    def z_copy(h, p, start):
        return remote(zs.at[h, p], z_in.at[h, p], z_s.at[h, p], z_r.at[h, p], zdev(p + 1), start)

    def to_z(h):
        sib_copy(h, False).wait_recv()
        for p in range(nz):
            zs[h, p] = (part[h, zat(p + 1), core] + sib_in[h, zat(p + 1)].astype(F32)).astype(BF16)
            if p + 1 < nz:
                z_copy(h, p, True)

    def f_copy(h, j, start):
        block = fin.at[h, x] if start else fin.at[h, xat(-j)]
        return remote(block, block, f_s.at[h, j - 1], f_r.at[h, j - 1], xdev(j), start)

    def from_z(h):
        total = zs[h, nz - 1].astype(F32)
        for p in range(nz - 1):
            z_copy(h, p, False).wait_recv()
            total += z_in[h, p].astype(F32)
        fin[h, x] = total.astype(BF16)
        for j in range(1, nx):
            f_copy(h, j, True)

    with jax.named_scope("att_2"):
        att_wait(1)
    with jax.named_scope("part_0"):
        other_parts(0)
    with jax.named_scope("att_3"):
        att_wait(2)
    with jax.named_scope("to_z_0"):
        to_z(0)
    with jax.named_scope("part_1"):
        other_parts(1)
    with jax.named_scope("att_4"):
        att_wait(3)
    with jax.named_scope("to_z_1"):
        to_z(1)
    with jax.named_scope("from_z_0"):
        from_z(0)
    with jax.named_scope("mixed"):
        for k in (0, 1, -1, 2, -2, 3, -3):
            mix(k)
        att_wait(4)
        mix(4)
        mixed_o[...] = acc[...].astype(BF16)
    with jax.named_scope("from_z"):
        for h in range(1, heads):
            from_z(h)
    with jax.named_scope("from_x"):
        for h in range(heads):
            for j in range(1, nx):
                f_copy(h, j, False).wait_recv()
            grad_o[:, pl.ds(h * HEAD_DIM, HEAD_DIM)] = fin[h].reshape(wide, HEAD_DIM)
    with jax.named_scope("drain"):
        for copy in sent + [
            c for ring in (*out_w.rings, *kv_w.rings, query_ring, *pick_rings, *att_rings) for c in ring.sent
        ]:
            copy.wait_send()


def shards(sizes, hidden, states, owner, query_w, key_w, value_w, out_w, cotangent):
    cores, nz, nx, ny = sizes
    tok, wide = hidden.shape
    slots, length, enc_d = states.shape
    spans, per = owner.shape
    proj = query_w.shape[1]
    heads = proj // HEAD_DIM
    n_dp = cores * nz
    used = spans * per
    piece = length // ny
    pairs = used * piece
    cols = out_w.shape[1]
    keys = per * length
    padded = tok + tok // spans
    dma = pltpu.SemaphoreType.DMA
    any_, vmem = pl.BlockSpec(memory_space=pltpu.HBM), pl.BlockSpec(memory_space=pltpu.VMEM)
    block = wide // n_dp
    quarter = block // nx
    scratch = [
        pltpu.SMEM((per, spans), jnp.int32),
        pltpu.VMEM((tok, wide), BF16),
        pltpu.VMEM((tok, cols), BF16),
        pltpu.VMEM(key_w.shape, BF16),
        pltpu.VMEM(key_w.shape, BF16),
        pltpu.VMEM((nz, cores, block, proj), BF16),
        pltpu.VMEM((n_dp * out_w.shape[0], cols), BF16),
        pltpu.VMEM((2 * enc_d, proj), BF16),
        pltpu.VMEM((enc_d, 2 * proj), F32),
        pltpu.VMEM((enc_d, 2 * proj), BF16),
        pltpu.VMEM((ny, slots, piece, enc_d // 256 * 128 + 128), BF16),
        pltpu.VMEM((ny, slots, piece, enc_d - enc_d // 256 * 128 - 128), BF16),
        pltpu.VMEM((ny, pairs, enc_d), BF16),
        pltpu.VMEM((spans + 1, keys, 2 * proj), BF16),
        pltpu.VMEM((ny, heads, tok, HEAD_DIM), BF16),
        pltpu.VMEM((2, ny // 2, heads, tok, HEAD_DIM), BF16),
        pltpu.VMEM((2, ny // 2, heads, tok, HEAD_DIM), BF16),
        pltpu.VMEM((padded, proj), F32),
        pltpu.VMEM((padded, proj), F32),
        pltpu.VMEM(((spans + 1) * heads, tok // spans, keys), F32),
        pltpu.VMEM((padded, proj), F32),
        pltpu.VMEM((ny, tok, proj), BF16),
        pltpu.VMEM((padded, proj), F32),
        pltpu.VMEM((nz, cores, block, tok), BF16),
        pltpu.VMEM((nx, nz, cores, quarter, tok), BF16),
        pltpu.VMEM((heads, nx, tok, HEAD_DIM), BF16),
        pltpu.VMEM((heads, nz, cores, quarter, HEAD_DIM), F32),
        pltpu.VMEM((heads, nz, quarter, HEAD_DIM), BF16),
        pltpu.VMEM((heads, nz, quarter, HEAD_DIM), BF16),
        pltpu.VMEM((heads, nz, quarter, HEAD_DIM), BF16),
        pltpu.VMEM((heads, nz - 1, quarter, HEAD_DIM), BF16),
        pltpu.VMEM((heads, nx, quarter, HEAD_DIM), BF16),
        pltpu.VMEM((tok, cols), F32),
        dma((9,)),
        dma((2, ny - 1)), dma((2, ny - 1)),
        dma((2, 2, ny // 2)), dma((2, 2, ny // 2)),
        dma((2, 2, ny // 2)), dma((2, 2, ny // 2)),
        dma((2, 2, ny // 2)), dma((2, 2, ny // 2)),
        dma((2, 2, nz // 2)), dma((2, 2, nz // 2)),
        dma((2, nz // 2)), dma((2, nz // 2)),
        dma((1, 2, nz // 2)), dma((1, 2, nz // 2)),
        dma((nz,)), dma((nz,)), dma(()), dma(()), dma((nz,)), dma((nz,)),
        dma((nz - 1, nx - 1)), dma((nz - 1, nx - 1)),
        dma((ny,)), dma((ny,)),
        dma((nx - 1,)), dma((nx - 1,)),
        dma((heads, nx - 1)), dma((heads, nx - 1)),
        dma((heads,)), dma((heads,)),
        dma((heads, nz - 1)), dma((heads, nz - 1)),
        dma((heads, nx - 1)), dma((heads, nx - 1)),
    ]
    operands = [
        pltpu.with_memory_space_constraint(a, pltpu.HBM)
        for a in (hidden, states, owner.T, query_w, key_w, value_w, out_w, cotangent)
    ]
    mixed, grad = pl.pallas_call(
        functools.partial(kernel, cores, nz, nx, ny, spans),
        out_shape=(
            jax.ShapeDtypeStruct((tok, cols), BF16),
            jax.ShapeDtypeStruct((wide // n_dp, proj), BF16),
        ),
        in_specs=[any_, any_, any_, any_, any_, any_, any_, any_],
        out_specs=(vmem, vmem),
        scratch_shapes=scratch,
        compiler_params=pltpu.CompilerParams(
            collective_id=0, has_side_effects=True, vmem_limit_bytes=48 * 2**20
        ),
        cost_estimate=pl.CostEstimate(flops=3 * 10**9, bytes_accessed=8 * 2**20, transcendentals=163840),
    )(*operands)
    return mixed, grad.astype(F32)


def solution(mesh):
    sizes = (2, mesh.shape["dp"] // 2, mesh.shape["ctx"], mesh.shape["enc"])
    in_specs = (
        P(("dp", "ctx"), None),
        P(("dp", "ctx", "enc"), None, None),
        P(("dp", "ctx"), None),
        P("dp", "enc"),
        P("dp", "enc"),
        P("dp", "enc"),
        P("dp", "enc"),
        P(("dp", "ctx"), "enc"),
    )
    out_specs = (P(("dp", "ctx"), "enc"), P("dp", "enc"))
    return jax.shard_map(
        functools.partial(shards, sizes),
        mesh=mesh,
        in_specs=in_specs,
        out_specs=out_specs,
        check_vma=False,
    )
```
